512 devices in a mesh: dp: 8 (over x, core), expert: 64 (over z, y).
Axes of the slice: x: 4, y: 4, z: 16, core: 2. Of those that a mesh axis runs over, the one named last changes fastest.
Arguments:
- x_stash: bfloat16 [8192, 1440], P('expert', 'dp'), may hold values from -6 to 6
- out_grad: bfloat16 [8192, 1440], P('expert', 'dp'), may hold values from -6 to 6
- expert_ids: int32 [4, 8192], replicated, may hold values from 0 to 63, as said below
- gates: float32 [4, 8192], replicated, may hold values from 0.1 to 1
- scales: float32 [8192], replicated, may hold values from 0.25 to 4
- w_gate: bfloat16 [64, 1440, 2048], P('expert', None, 'dp'), may hold values from -0.15625 to 0.15625
- w_up: bfloat16 [64, 1440, 2048], P('expert', None, 'dp'), may hold values from -0.15625 to 0.15625
- w_down: bfloat16 [64, 2048, 1440], P('expert', 'dp'), may hold values from -0.125 to 0.125
Outputs:
- grad_input: bfloat16 [8192, 1440], P('expert', 'dp')
- grad_gate: bfloat16 [64, 1440, 2048], P('expert', None, 'dp')
- grad_up: bfloat16 [64, 1440, 2048], P('expert', None, 'dp')
- grad_down: bfloat16 [64, 2048, 1440], P('expert', 'dp')
The draws below stay inside these ranges and needn't reach their ends.
Inputs may be any that keep to these rules, and one draw needn't show every extreme that they name: `expert_ids`: each token names 4 different experts. In each aligned block of 128 tokens, no expert is named by more than 16 tokens, and some expert is named by exactly 16 tokens of some block.
All inputs are finite; a program needn't handle non-finite values.
Results may differ from the reference program's by a relative error of at most 0.02.
Values may be sent and summed in bfloat16 or wider, within the bound.
A program may use at most 64 MiB of HBM per device.

```python
import math
import jax
import jax.numpy as jnp
from jax import lax

D = 1440
FF = 2048
TOP = 4
TOK_DEV = 128
EXPERTS = 64
TOKENS = 8192
N_DP = 8


def draw_expert_ids(key, part):
    key = jax.random.fold_in(key, 11)
    blocks = TOKENS // TOK_DEV
    first, second, third = jax.random.split(key, 3)
    perms = jax.vmap(lambda k: jax.random.permutation(k, EXPERTS))(jax.random.split(first, blocks))
    orders = jax.vmap(lambda k: jax.random.permutation(k, TOK_DEV))(jax.random.split(second, blocks))
    halves = jax.random.randint(third, (blocks,), 0, 2).astype(jnp.int32)
    halves = halves.at[0].set(1)
    cycle = jnp.where(halves == 1, EXPERTS // 2, EXPERTS).astype(jnp.int32)
    entry = orders[:, :, None].astype(jnp.int32) * TOP + jnp.arange(TOP, dtype=jnp.int32)[None, None, :]
    places = entry % cycle[:, None, None]
    chosen = jnp.take_along_axis(perms.astype(jnp.int32), places.reshape(blocks, TOK_DEV * TOP), axis=1)
    chosen = chosen.reshape(blocks, TOK_DEV, TOP)
    return jnp.transpose(chosen, (2, 0, 1)).reshape(TOP, TOKENS).astype(jnp.int32)


def levels(own_key, dims, shards, smallest, high):
    level, own = 1.0, jax.random.fold_in(own_key, 6)
    for axis_at, parts in shards:
        draws = jnp.exp(jax.random.uniform(jax.random.fold_in(own, axis_at), (parts,), jnp.float32, smallest / len(shards), high / len(shards)))
        level = level * jnp.repeat(draws, dims[axis_at] // parts).reshape([-1 if axis == axis_at else 1 for axis in range(len(dims))])
    return level


def gaussian(stream_key, extent, spread, reach, cuts=(), kind=jnp.bfloat16):
    drawn = spread * jax.random.normal(stream_key, extent, jnp.float32)
    if cuts:
        drawn = drawn * levels(stream_key, extent, cuts, -0.22, 0.18)
    return jnp.clip(drawn, -reach, reach).astype(kind)


def setup_inputs(seed: int = 0) -> dict:
    key_list = jax.random.split(jax.random.key(seed), 9)
    return {
        "x_stash": gaussian(key_list[0], (TOKENS, D), 1.0, 6.0, ((0, 64), (1, 8))),
        "out_grad": gaussian(key_list[1], (TOKENS, D), 1.0, 6.0, ((0, 64), (1, 8))),
        "expert_ids": draw_expert_ids(jax.random.fold_in(key_list[8], 71), 0),
        "gates": jnp.clip(jax.random.uniform(key_list[3], (TOP, TOKENS), jnp.float32, 0.1, 1.0), 0.1, 1.0),
        "scales": jnp.clip(jnp.exp(jax.random.uniform(key_list[4], (TOKENS,), jnp.float32, math.log(0.25), math.log(4.0))), 0.25, 4.0),
        "w_gate": gaussian(key_list[5], (EXPERTS, D, FF), D ** -0.5, 0.15625, ((0, 64), (2, 8))),
        "w_up": gaussian(key_list[6], (EXPERTS, D, FF), D ** -0.5, 0.15625, ((0, 64), (2, 8))),
        "w_down": gaussian(key_list[7], (EXPERTS, FF, D), FF ** -0.5, 0.125, ((0, 64), (1, 8))),
    }


def reference(x_stash, out_grad, expert_ids, gates, scales, w_gate, w_up, w_down):
    tokens, width = x_stash.shape
    experts = w_gate.shape[0]
    hidden = w_gate.shape[2]
    blocks = tokens // TOK_DEV
    slots_per = 2 * TOK_DEV * TOP // experts
    group = hidden // N_DP
    x_full = (x_stash.astype(jnp.float32) * scales[:, None]).astype(jnp.bfloat16)
    starts = (jnp.arange(blocks, dtype=jnp.int32) * TOK_DEV)[:, None, None]
    position = jnp.arange(TOK_DEV, dtype=jnp.int32)[None, None, :]
    slot_iota = jnp.arange(slots_per, dtype=jnp.int32)[None, :, None]

    def one_expert(carry, inputs):
        expert, wg, wu, wd = inputs
        named = expert_ids == expert
        weight = jnp.sum(jnp.where(named, gates, jnp.float32(0.0)), axis=0).reshape(blocks, TOK_DEV)
        hit = jnp.any(named, axis=0).astype(jnp.int32).reshape(blocks, TOK_DEV)
        rank = jnp.cumsum(hit, axis=1, dtype=jnp.int32) - hit
        onehot = ((rank[:, None, :] == slot_iota) & (hit[:, None, :] == 1)).astype(jnp.int32)
        rows = jnp.sum(onehot * (starts + position), axis=2, dtype=jnp.int32).reshape(-1)
        gate = jnp.sum(onehot.astype(jnp.float32) * weight[:, None, :], axis=2).reshape(-1)
        valid = jnp.sum(onehot, axis=2, dtype=jnp.int32).reshape(-1).astype(jnp.float32)
        xs = x_full[rows]
        dys = out_grad[rows]
        g = jnp.dot(xs, wg, preferred_element_type=jnp.float32)
        u = jnp.dot(xs, wu, preferred_element_type=jnp.float32)
        sig = jax.nn.sigmoid(g)
        act = (gate[:, None] * (g * sig * u)).astype(jnp.bfloat16)
        dsum = jnp.dot(dys, wd.T, preferred_element_type=jnp.float32)
        d_a = gate[:, None] * dsum
        d_gate = (d_a * u * sig * (1.0 + g * (1.0 - sig))).astype(jnp.bfloat16)
        d_up = (d_a * g * sig).astype(jnp.bfloat16)
        grad_down = jnp.dot(act.T, dys, preferred_element_type=jnp.float32).astype(jnp.bfloat16)
        grad_gate = jnp.dot(xs.T, d_gate, preferred_element_type=jnp.float32).astype(jnp.bfloat16)
        grad_up = jnp.dot(xs.T, d_up, preferred_element_type=jnp.float32).astype(jnp.bfloat16)
        count = rows.shape[0]
        pieces = jnp.einsum("sjh,djh->jsd", d_gate.astype(jnp.float32).reshape(count, N_DP, group),
                            wg.astype(jnp.float32).reshape(width, N_DP, group), precision=lax.Precision.HIGHEST)
        pieces = pieces + jnp.einsum("sjh,djh->jsd", d_up.astype(jnp.float32).reshape(count, N_DP, group),
                                     wu.astype(jnp.float32).reshape(width, N_DP, group), precision=lax.Precision.HIGHEST)
        contrib = jnp.sum(pieces.astype(jnp.bfloat16).astype(jnp.float32), axis=0)
        carry = carry.at[rows].add(contrib * valid[:, None])
        return carry, (grad_gate, grad_up, grad_down)

    start = jnp.zeros((tokens, width), dtype=jnp.float32)
    ids = jnp.arange(experts, dtype=jnp.int32)
    total, grads = lax.scan(one_expert, start, (ids, w_gate, w_up, w_down))
    return total.astype(jnp.bfloat16), grads[0], grads[1], grads[2]
```

```python
import jax
import jax.numpy as jnp
from jax import lax
from jax.experimental import pallas as pl
from jax.experimental.pallas import tpu as pltpu
from jax.sharding import PartitionSpec as P

TOP = 4
NX, NY, NZ = 4, 4, 16
CHUNKS = NZ // 2
TOK = 128
SLOTS = 16
FEAT = 180
WIDE = 384
HID = 256
HALF = NY * SLOTS
ROWS = 2 * HALF
LAG = 7
F32 = jnp.float32
BF16 = jnp.bfloat16


def kernel(
    tok, sel, gate, back_hot, w_gu, w_d, w_in,
    sum_out, ggu_out, gd_out,
    zp, zm, yb, g, dbuf, abuf, pb, sb, q, rl, rr, fl, fr, back, ret, fin,
    zp_s, zp_r, zm_s, zm_r, y_s, y_r, xr_s, xr_r, xl_s, xl_r, xfr_s, xfr_r, xfl_s, xfl_r,
    sib_s, sib_r, ps_s, ps_r, ar_s, ar_r, al_s, al_r, br_s, br_r, bl_s, bl_r,
    ret_s, ret0_s, ret_r, fin_s, fin_r,
):
    dp = lax.axis_index("dp")
    ex = lax.axis_index("expert")
    x, c = dp // 2, dp % 2
    z, y = ex // NY, ex % NY
    oc = 1 - c
    xr, xl, xo = (x + 1) % NX, (x + NX - 1) % NX, (x + 2) % NX

    def dev(x_, c_, y_, z_):
        return {"dp": x_ * 2 + c_, "expert": z_ * NY + y_}

    zright, zleft = dev(x, c, y, (z + 1) % NZ), dev(x, c, y, (z + NZ - 1) % NZ)
    xright, xleft = dev(xr, c, y, z), dev(xl, c, y, z)
    sibling = dev(x, oc, y, z)

    def ret_z(i):
        return jnp.where(c == 0, z + NZ - i, z + i + 1) % NZ

    def ret_from(i):
        return jnp.where(c == 0, z + i, z + NZ - i - 1) % NZ

    def rc(src, dst, s, r, to):
        return pltpu.make_async_remote_copy(
            src_ref=src, dst_ref=dst, send_sem=s, recv_sem=r, device_id=to,
            device_id_type=pl.DeviceIdType.MESH,
        )

    def take(ref, sem):
        pltpu.make_async_copy(ref, ref, sem).wait()

    barrier = pltpu.get_barrier_semaphore()
    for to in (zright, zleft, xright, xleft, sibling):
        pl.semaphore_signal(barrier, inc=1, device_id=to, device_id_type=pl.DeviceIdType.MESH)
    for d in range(1, NY):
        pl.semaphore_signal(
            barrier, inc=1, device_id=dev(x, c, (y + d) % NY, z),
            device_id_type=pl.DeviceIdType.MESH,
        )

    @pl.loop(0, CHUNKS)
    def _(i):
        for d in range(NY):
            def send_signal():
                pl.semaphore_signal(
                    barrier, inc=1, device_id=dev(x, c, (y + d) % NY, ret_from(i)),
                    device_id_type=pl.DeviceIdType.MESH,
                )

            if d == 0:
                pl.when((c == 1) | (i > 0))(send_signal)
            else:
                send_signal()

    pl.semaphore_wait(barrier, 8 + CHUNKS * NY - jnp.where(c == 0, 1, 0))

    def z_right(i):
        return rc(zp.at[i], zp.at[i + 1], zp_s.at[i], zp_r.at[i + 1], zright)

    def z_left(i):
        return rc(zm.at[i], zm.at[i + 1], zm_s.at[i], zm_r.at[i + 1], zleft)

    first_left = rc(tok, zm.at[0], zm_s.at[CHUNKS - 1], zm_r.at[0], zleft)
    first_right = rc(tok, zp.at[1], zp_s.at[0], zp_r.at[1], zright)
    first_left.start()
    first_right.start()
    zp[0] = tok[...]

    def slot_rows(which):
        return pl.ds(pl.multiple_of(which * SLOTS, SLOTS), SLOTS)

    def y_send(i, d):
        to = (y + d) % NY
        return rc(
            yb.at[i, :, slot_rows(to), :], g.at[c, x, i, :, slot_rows(y), :],
            y_s.at[i], y_r.at[i], dev(x, c, to, z),
        )

    def stage_z(i):
        take(zm.at[i], zm_r.at[i])

        @pl.when(i < CHUNKS - 1)
        def _():
            z_left(i).start()

        @pl.when(i > 0)
        def _():
            take(zp.at[i], zp_r.at[i])

            @pl.when(i < CHUNKS - 1)
            def _():
                z_right(i).start()

        for h, src in ((0, zp), (1, zm)):
            yb[i, h] = jnp.dot(sel[i, h], src[i], preferred_element_type=F32).astype(BF16)
        for d in range(1, NY):
            y_send(i, d).start()
        pltpu.make_async_copy(
            yb.at[i, :, slot_rows(y), :], g.at[c, x, i, :, slot_rows(y), :], y_r.at[i]
        ).start()

    def sib_send(i, x_):
        return rc(g.at[c, x_, i], g.at[c, x_, i], sib_s.at[i], sib_r.at[i], sibling)

    def x_right(i):
        return rc(g.at[c, x, i], g.at[c, x, i], xr_s.at[i], xr_r.at[i], xright)

    def x_left(i):
        return rc(g.at[c, x, i], g.at[c, x, i], xl_s.at[i], xl_r.at[i], xleft)

    def x_far_right(i):
        return rc(g.at[c, xl, i, 0], g.at[c, xl, i, 0], xfr_s.at[i], xfr_r.at[i], xright)

    def x_far_left(i):
        return rc(g.at[c, xr, i, 1], g.at[c, xr, i, 1], xfl_s.at[i], xfl_r.at[i], xleft)

    def stage_x1(i):
        take(g.at[c, x, i], y_r.at[i])
        x_right(i).start()
        x_left(i).start()
        sib_send(i, x).start()

    def stage_x2(i):
        take(g.at[c, xl, i], xr_r.at[i])
        x_far_right(i).start()
        take(g.at[c, xr, i], xl_r.at[i])
        x_far_left(i).start()
        sib_send(i, xl).start()
        sib_send(i, xr).start()

    def stage_x3(i):
        take(g.at[c, xo, i, 0], xfr_r.at[i])
        take(g.at[c, xo, i, 1], xfl_r.at[i])
        sib_send(i, xo).start()

    def p_send(i):
        return rc(pb.at[i, oc], sb.at[i], ps_s.at[i], ps_r.at[i], sibling)

    def stage_c(i):
        take(g.at[oc, :, i], sib_r.at[i])
        blocks = [g[c_, x_, i].reshape(ROWS, WIDE) for c_ in range(2) for x_ in range(NX)]
        low = jnp.concatenate([b[:, :HID] for b in blocks], axis=1)
        high = jnp.concatenate([b[:, WIDE - HID :] for b in blocks], axis=1)
        gu = jnp.dot(low, w_gu[...], preferred_element_type=F32)
        h = jnp.dot(high, w_d[...], preferred_element_type=F32)
        p = gate[i]
        gg, u = gu[:, :HID], gu[:, HID:]
        s = jax.nn.sigmoid(gg)
        gs = gg * s
        h = p * h
        abuf[i] = (p * gs * u).astype(BF16)
        d_gate = (h * u * s * (1.0 + gg * (1.0 - s))).astype(BF16)
        d_up = (h * gs).astype(BF16)
        dd = jnp.concatenate([d_gate, d_up], axis=1)
        dbuf[i] = dd
        for x_ in range(NX):
            piece = jnp.dot(dd, w_in[x_], preferred_element_type=F32).astype(BF16)
            pb[i, 0, x_] = piece[:HALF]
            pb[i, 1, x_] = piece[HALF:]
        p_send(i).start()

    quarter = HALF // 2

    def a_right(i):
        return rc(q.at[i, xo, pl.ds(0, quarter)], rl.at[i], ar_s.at[i], ar_r.at[i], xright)

    def a_left(i):
        return rc(q.at[i, xo, pl.ds(quarter, quarter)], rr.at[i], al_s.at[i], al_r.at[i], xleft)

    def b_right(i):
        return rc(q.at[i, xr], fl.at[i], br_s.at[i], br_r.at[i], xright)

    def b_left(i):
        return rc(q.at[i, xl], fr.at[i], bl_s.at[i], bl_r.at[i], xleft)

    def stage_r1(i):
        take(sb.at[i], ps_r.at[i])
        q[i] = (pb[i, c].astype(F32) + sb[i].astype(F32)).astype(BF16)
        a_right(i).start()
        a_left(i).start()

    def stage_r2(i):
        take(rl.at[i], ar_r.at[i])
        lo, hi = pl.ds(0, quarter), pl.ds(quarter, quarter)
        q[i, xr, lo] = (q[i, xr, lo].astype(F32) + rl[i].astype(F32)).astype(BF16)
        b_right(i).start()
        take(rr.at[i], al_r.at[i])
        q[i, xl, hi] = (q[i, xl, hi].astype(F32) + rr[i].astype(F32)).astype(BF16)
        b_left(i).start()

    def ret_send(i, d, sem):
        to = (y + d) % NY
        return rc(
            back.at[i, slot_rows(to), :], ret.at[i, slot_rows(y), :],
            sem, ret_r, dev(x, c, to, ret_z(i)),
        )

    def stage_r3(i):
        take(fl.at[i], br_r.at[i])
        take(fr.at[i], bl_r.at[i])
        back[i] = (q[i, x].astype(F32) + fl[i].astype(F32) + fr[i].astype(F32)).astype(BF16)
        for d in range(1, NY):
            ret_send(i, d, ret_s.at[i]).start()
        local = (c == 0) & (i == 0)

        @pl.when(local)
        def _():
            pltpu.make_async_copy(
                back.at[i, slot_rows(y), :], ret.at[i, slot_rows(y), :], ret_r
            ).start()

        @pl.when(jnp.logical_not(local))
        def _():
            ret_send(i, 0, ret0_s.at[i]).start()

    stages = (
        (stage_z, 0), (stage_x1, 1), (stage_x2, 2), (stage_x3, 3),
        (stage_c, 4), (stage_r1, 5), (stage_r2, 6), (stage_r3, 7),
    )

    @pl.loop(0, CHUNKS + LAG)
    def _(step):
        for stage, lag in stages:
            i = step - lag

            @pl.when((i >= 0) & (i < CHUNKS))
            def _():
                stage(i)

    first = (((0,), (0,)), ((), ()))
    rows = CHUNKS * ROWS

    @pl.loop(0, 2)
    def _(c_):
        @pl.loop(0, NX)
        def _(x_):
            own = g[c_, x_].reshape(rows, WIDE)
            dd = dbuf[...].reshape(rows, 2 * HID)
            ggu_out[x_, c_] = lax.dot_general(
                own[:, :HID], dd, first, preferred_element_type=F32
            )[: ggu_out.shape[2]].astype(BF16)
            aa = abuf[...].reshape(rows, HID)
            gd_out[x_, c_] = lax.dot_general(
                aa, own[:, WIDE - HID :], first, preferred_element_type=F32
            ).astype(BF16)

    take(ret, ret_r)
    fin[0] = jnp.dot(back_hot[...], ret[...].reshape(CHUNKS * HALF, WIDE), preferred_element_type=F32)
    last = rc(fin.at[0], fin.at[1], fin_s, fin_r, sibling)
    last.start()

    @pl.loop(0, CHUNKS)
    def _(i):
        @pl.when(i < CHUNKS - 1)
        def _():
            z_left(i).wait_send()
            z_right(i).wait_send()

        take(yb.at[i, :, pl.ds(0, (NY - 1) * SLOTS), :], y_s.at[i])
        x_right(i).wait_send()
        x_left(i).wait_send()
        x_far_right(i).wait_send()
        x_far_left(i).wait_send()
        take(g.at[c, :, i], sib_s.at[i])
        p_send(i).wait_send()
        a_right(i).wait_send()
        a_left(i).wait_send()
        b_right(i).wait_send()
        b_left(i).wait_send()
        take(back.at[i, pl.ds(0, (NY - 1) * SLOTS), :], ret_s.at[i])

        @pl.when((c == 1) | (i > 0))
        def _():
            ret_send(i, 0, ret0_s.at[i]).wait_send()

    first_left.wait_send()
    last.wait()
    sum_out[...] = fin[0] + fin[1]


def one_hot(hit, tri):
    rank = jnp.dot(hit.astype(BF16), tri, preferred_element_type=F32).astype(jnp.int32)
    slot = lax.broadcasted_iota(jnp.int32, (SLOTS, 1), 0)
    return (rank[..., None, :] == slot) & hit[..., None, :]


def on_device(x_stash, out_grad, expert_ids, gates, scales, w_gate, w_up, w_down):
    dp = lax.axis_index("dp")
    ex = lax.axis_index("expert")
    c = dp % 2
    z, y = ex // NY, ex % NY

    scale = lax.dynamic_slice_in_dim(scales, ex * TOK, TOK, 0)
    xs = (x_stash.astype(F32) * scale[:, None]).astype(BF16)
    tok = jnp.concatenate([xs, out_grad, jnp.zeros((TOK, WIDE - 2 * FEAT), BF16)], axis=1)

    tri = (
        lax.broadcasted_iota(jnp.int32, (TOK, TOK), 0)
        < lax.broadcasted_iota(jnp.int32, (TOK, TOK), 1)
    ).astype(BF16)

    def relative(a):
        a = a.reshape(TOP, NZ, NY, TOK)
        a = jnp.concatenate([a, a], axis=1)
        low = lax.dynamic_slice_in_dim(a, z + NZ - CHUNKS + 1, CHUNKS, 1)[:, ::-1]
        high = lax.dynamic_slice_in_dim(a, z + 1, CHUNKS, 1)
        return jnp.stack([low, high], axis=2)

    ids = relative(expert_ids)
    weights = relative(gates)
    ids_y = lax.dynamic_index_in_dim(ids, y, 3, keepdims=False)
    experts = z * NY + jnp.arange(NY, dtype=jnp.int32)
    hit = jnp.any(ids_y[:, :, :, None, :] == experts[:, None], axis=0)
    sel = one_hot(hit, tri).astype(BF16).reshape(CHUNKS, 2, HALF, TOK)
    named = ids == ex
    weight = jnp.sum(jnp.where(named, weights, F32(0.0)), axis=0)
    mine = one_hot(jnp.any(named, axis=0), tri)
    gate = jnp.sum(jnp.where(mine, weight[..., None, :], F32(0.0)), axis=-1)
    gate = gate.reshape(CHUNKS, ROWS, 1)

    own_ids = lax.dynamic_slice_in_dim(expert_ids, ex * TOK, TOK, 1)
    step = jnp.arange(CHUNKS, dtype=jnp.int32)
    from_z = jnp.where(c == 0, z + step, z + NZ - 1 - step) % NZ
    senders = from_z[:, None] * NY + jnp.arange(NY, dtype=jnp.int32)
    sent = jnp.any(own_ids[:, None, None, :] == senders[:, :, None], axis=0)
    back_hot = one_hot(sent, tri).astype(BF16).reshape(CHUNKS * HALF, TOK).T

    def by_owner(w):
        w = w.reshape(NX, 2, FEAT, HID).transpose(1, 0, 2, 3)
        return jnp.pad(w, ((0, 0), (0, 0), (0, HID - FEAT), (0, 0))).reshape(2 * NX * HID, HID)

    w_gu = jnp.concatenate([by_owner(w_gate[0]), by_owner(w_up[0])], axis=1)
    shift = FEAT - (WIDE - HID)
    w_d = w_down[0].T.reshape(NX, 2, FEAT, HID).transpose(1, 0, 2, 3)
    w_d = jnp.pad(w_d, ((0, 0), (0, 0), (shift, HID - FEAT - shift), (0, 0)))
    w_d = w_d.reshape(2 * NX * HID, HID)

    def by_chip(w):
        w = w.reshape(NX, 2 * FEAT, HID).transpose(0, 2, 1)
        return jnp.pad(w, ((0, 0), (0, 0), (0, WIDE - 2 * FEAT)))

    w_in = jnp.concatenate([by_chip(w_gate[0]), by_chip(w_up[0])], axis=1)

    vmem = pl.BlockSpec(memory_space=pltpu.VMEM)
    keep = 192
    block = (CHUNKS, 2, HALF, WIDE)
    dma = pltpu.SemaphoreType.DMA
    per_chunk = dma((CHUNKS,))
    total, ggu, gd = pl.pallas_call(
        kernel,
        out_shape=(
            jax.ShapeDtypeStruct((TOK, WIDE), F32),
            jax.ShapeDtypeStruct((NX, 2, keep, 2 * HID), BF16),
            jax.ShapeDtypeStruct((NX, 2, HID, HID), BF16),
        ),
        in_specs=[vmem] * 7,
        out_specs=(vmem, vmem, vmem),
        scratch_shapes=[
            pltpu.VMEM((CHUNKS, TOK, WIDE), BF16),
            pltpu.VMEM((CHUNKS, TOK, WIDE), BF16),
            pltpu.VMEM(block, BF16),
            pltpu.VMEM((2, NX) + block, BF16),
            pltpu.VMEM((CHUNKS, ROWS, 2 * HID), BF16),
            pltpu.VMEM((CHUNKS, ROWS, HID), BF16),
            pltpu.VMEM((CHUNKS, 2, NX, HALF, WIDE), BF16),
            pltpu.VMEM((CHUNKS, NX, HALF, WIDE), BF16),
            pltpu.VMEM((CHUNKS, NX, HALF, WIDE), BF16),
            pltpu.VMEM((CHUNKS, HALF // 2, WIDE), BF16),
            pltpu.VMEM((CHUNKS, HALF // 2, WIDE), BF16),
            pltpu.VMEM((CHUNKS, HALF, WIDE), BF16),
            pltpu.VMEM((CHUNKS, HALF, WIDE), BF16),
            pltpu.VMEM((CHUNKS, HALF, WIDE), BF16),
            pltpu.VMEM((CHUNKS, HALF, WIDE), BF16),
            pltpu.VMEM((2, TOK, WIDE), F32),
        ]
        + [per_chunk] * 26
        + [per_chunk, per_chunk, dma, dma, dma],
        compiler_params=pltpu.CompilerParams(
            collective_id=0, has_side_effects=True, vmem_limit_bytes=56 * 1024 * 1024
        ),
    )(tok, sel, gate, back_hot, w_gu, w_d, w_in)

    grad_input = lax.dynamic_slice_in_dim(total, c * FEAT, FEAT, 1).astype(BF16)
    d = 2 * NX * FEAT
    grad_gate = ggu[:, :, :FEAT, :HID].reshape(d, HID)
    grad_up = ggu[:, :, :FEAT, HID:].reshape(d, HID)
    grad_down = gd[:, :, :, shift : shift + FEAT].transpose(2, 0, 1, 3).reshape(HID, d)
    return grad_input, grad_gate[None], grad_up[None], grad_down[None]


def solution(mesh):
    return jax.shard_map(
        on_device,
        mesh=mesh,
        in_specs=(
            P("expert", "dp"),
            P("expert", "dp"),
            P(),
            P(),
            P(),
            P("expert", None, "dp"),
            P("expert", None, "dp"),
            P("expert", "dp", None),
        ),
        out_specs=(
            P("expert", "dp"),
            P("expert", None, "dp"),
            P("expert", None, "dp"),
            P("expert", "dp", None),
        ),
        check_vma=False,
    )
```

```python
import jax
import jax.numpy as jnp
from jax import lax
from jax.experimental import pallas as pl
from jax.experimental.pallas import tpu as pltpu
from jax.sharding import PartitionSpec as P

TOP = 4
NX, NY, NZ = 4, 4, 16
CHUNKS = NZ // 2
TOK = 128
SLOTS = 16
FEAT = 180
WIDE = 384
HID = 256
HALF = NY * SLOTS
ROWS = 2 * HALF
LAG = 7
F32 = jnp.float32
BF16 = jnp.bfloat16


def one_hot(hit, rows):
    tri = (
        lax.broadcasted_iota(jnp.int32, (TOK, TOK), 0)
        < lax.broadcasted_iota(jnp.int32, (TOK, TOK), 1)
    ).astype(BF16)
    rank = jnp.dot(hit.astype(BF16), tri, preferred_element_type=F32)
    code = jnp.where(hit > 0.0, rank, F32(-1.0))
    code = jnp.broadcast_to(code[:, None, :], (rows, SLOTS, TOK)).reshape(rows * SLOTS, TOK)
    slot = lax.broadcasted_iota(jnp.int32, (rows * SLOTS, TOK), 0) & (SLOTS - 1)
    return code == slot.astype(F32)


def far(i):
    return (i >> 1) + (CHUNKS // 2) * (i & 1)


def kernel(
    x_in, dy_in, ids, gates, scales, wg_hbm, wu_hbm, wd_hbm,
    gi_out, gg_out, gu_out, gd_out,
    wg, wu, wdt, w_in, sel, gate, xs_buf, dy_buf,
    zp, zm, yb, g, dgbuf, dubuf, abuf, pb, sb, q, rl, rr, fl, fr, back, ret, fin,
    w_sem, zp_s, zp_r, zm_s, zm_r, y_s, y_r, xr_s, xr_r, xl_s, xl_r, xfr_s, xfr_r, xfl_s, xfl_r,
    sib_s, sib_r, ps_s, ps_r, ar_s, ar_r, al_s, al_r, br_s, br_r, bl_s, bl_r,
    ret_s, ret0_s, ret_r, fin_s, fin_r,
):
    dp = lax.axis_index("dp")
    ex = lax.axis_index("expert")
    x, c = dp // 2, dp % 2
    z, y = ex // NY, ex % NY
    oc = 1 - c
    xr, xl, xo = (x + 1) % NX, (x + NX - 1) % NX, (x + 2) % NX

    def dev(x_, c_, y_, z_):
        return {"dp": x_ * 2 + c_, "expert": z_ * NY + y_}

    zright, zleft = dev(x, c, y, (z + 1) % NZ), dev(x, c, y, (z + NZ - 1) % NZ)
    xright, xleft = dev(xr, c, y, z), dev(xl, c, y, z)
    sibling = dev(x, oc, y, z)

    def ret_z(i):
        return jnp.where(c == 0, z + NZ - far(i), z + far(i) + 1) % NZ

    def ret_from(i):
        return jnp.where(c == 0, z + far(i), z + NZ - far(i) - 1) % NZ

    def rc(src, dst, s, r, to):
        return pltpu.make_async_remote_copy(
            src_ref=src, dst_ref=dst, send_sem=s, recv_sem=r, device_id=to,
            device_id_type=pl.DeviceIdType.MESH,
        )

    def take(ref, sem):
        pltpu.make_async_copy(ref, ref, sem).wait()

    jump = CHUNKS // 2
    express_right = dev(x, c, y, (z + jump) % NZ)
    express_left = dev(x, c, y, (z + NZ - jump - 1) % NZ)
    weights = [
        pltpu.make_async_copy(src, dst, w_sem.at[n])
        for n, (src, dst) in enumerate(((wg_hbm, wg), (wu_hbm, wu), (wd_hbm, wdt)))
    ]
    for copy in weights:
        copy.start()

    barrier = pltpu.get_barrier_semaphore()
    for to in (
        zright, zleft, xright, xleft, sibling,
        dev(x, c, y, (z + NZ - jump) % NZ), dev(x, c, y, (z + jump + 1) % NZ),
    ):
        pl.semaphore_signal(barrier, inc=1, device_id=to, device_id_type=pl.DeviceIdType.MESH)
    for d in range(1, NY):
        pl.semaphore_signal(
            barrier, inc=1, device_id=dev(x, c, (y + d) % NY, z),
            device_id_type=pl.DeviceIdType.MESH,
        )

    @pl.loop(0, CHUNKS)
    def _(i):
        for d in range(NY):
            def send_signal():
                pl.semaphore_signal(
                    barrier, inc=1, device_id=dev(x, c, (y + d) % NY, ret_from(i)),
                    device_id_type=pl.DeviceIdType.MESH,
                )

            if d == 0:
                pl.when((c == 1) | (i > 0))(send_signal)
            else:
                send_signal()

    xs_own = (x_in[...].astype(F32) * scales[pl.ds(ex, 1), :]).astype(BF16).astype(F32)
    own = [xs_own, dy_in[...].astype(F32), jnp.zeros((WIDE - 2 * FEAT, TOK), F32)]
    zp[0] = jnp.concatenate(own, axis=0).astype(BF16).T

    pl.semaphore_wait(barrier, 10 + CHUNKS * NY - jnp.where(c == 0, 1, 0))

    def z_right(i):
        return rc(zp.at[i], zp.at[i + 2], zp_s.at[i], zp_r.at[i + 2], zright)

    def z_left(i):
        return rc(zm.at[i], zm.at[i + 2], zm_s.at[i], zm_r.at[i + 2], zleft)

    first = (
        rc(zp.at[0], zp.at[2], zp_s.at[0], zp_r.at[2], zright),
        rc(zp.at[0], zm.at[0], zm_s.at[CHUNKS - 1], zm_r.at[0], zleft),
        rc(zp.at[0], zp.at[1], zp_s.at[CHUNKS - 1], zp_r.at[1], express_right),
        rc(zp.at[0], zm.at[1], zm_s.at[CHUNKS - 2], zm_r.at[1], express_left),
    )
    for copy in first:
        copy.start()

    def origins(i):
        return (z + NZ - far(i)) % NZ, (z + far(i) + 1) % NZ

    def prepare_sel(i):
        expert = z * NY + lax.broadcasted_iota(jnp.int32, (NY, TOK), 0)
        hits = []
        for zo in origins(i):
            block = ids[zo * NY + y]
            hit = jnp.zeros((NY, TOK), F32)
            for k in range(TOP):
                hit = hit + jnp.where(block[k : k + 1] == expert, F32(1.0), F32(0.0))
            hits.append(hit)
        hot = one_hot(jnp.concatenate(hits, axis=0), 2 * NY)
        sel[i] = jnp.where(hot, F32(1.0), F32(0.0)).astype(BF16)

    def prepare_gate(i):
        hits, weight = [], []
        for zo in origins(i):
            for ys in range(NY):
                named = ids[zo * NY + ys] == ex
                hits.append(jnp.sum(jnp.where(named, F32(1.0), F32(0.0)), axis=0, keepdims=True))
                weight.append(
                    jnp.sum(
                        jnp.where(named, gates[zo * NY + ys], F32(0.0)), axis=0, keepdims=True
                    )
                )
        hot = one_hot(jnp.concatenate(hits, axis=0), 2 * NY)
        w = jnp.concatenate(weight, axis=0)
        w = jnp.broadcast_to(w[:, None, :], (2 * NY, SLOTS, TOK)).reshape(ROWS, TOK)
        gate[i] = jnp.sum(jnp.where(hot, w, F32(0.0)), axis=1, keepdims=True)

    pl.loop(0, CHUNKS)(prepare_sel)

    def slot_rows(which):
        return pl.ds(pl.multiple_of(which * SLOTS, SLOTS), SLOTS)

    def y_send(i, d):
        to = (y + d) % NY
        return rc(
            yb.at[i, :, slot_rows(to), :], g.at[c, x, i, :, slot_rows(y), :],
            y_s.at[i], y_r.at[i], dev(x, c, to, z),
        )

    def stage_z(i):
        take(zm.at[i], zm_r.at[i])

        @pl.when(i < CHUNKS - 2)
        def _():
            z_left(i).start()

        @pl.when(i > 0)
        def _():
            take(zp.at[i], zp_r.at[i])

            @pl.when(i < CHUNKS - 2)
            def _():
                z_right(i).start()

        for h, src in ((0, zp), (1, zm)):
            yb[i, h] = jnp.dot(
                sel[i, pl.ds(h * HALF, HALF)], src[i], preferred_element_type=F32
            ).astype(BF16)
        for d in range(1, NY):
            y_send(i, d).start()
        pltpu.make_async_copy(
            yb.at[i, :, slot_rows(y), :], g.at[c, x, i, :, slot_rows(y), :], y_r.at[i]
        ).start()

    def sib_send(i, x_):
        return rc(g.at[c, x_, i], g.at[c, x_, i], sib_s.at[i], sib_r.at[i], sibling)

    def x_right(i):
        return rc(g.at[c, x, i], g.at[c, x, i], xr_s.at[i], xr_r.at[i], xright)

    def x_left(i):
        return rc(g.at[c, x, i], g.at[c, x, i], xl_s.at[i], xl_r.at[i], xleft)

    def x_far_right(i):
        return rc(g.at[c, xl, i, 0], g.at[c, xl, i, 0], xfr_s.at[i], xfr_r.at[i], xright)

    def x_far_left(i):
        return rc(g.at[c, xr, i, 1], g.at[c, xr, i, 1], xfl_s.at[i], xfl_r.at[i], xleft)

    def stage_x1(i):
        take(g.at[c, x, i], y_r.at[i])
        x_right(i).start()
        x_left(i).start()
        sib_send(i, x).start()

    def stage_x2(i):
        take(g.at[c, xl, i], xr_r.at[i])
        x_far_right(i).start()
        take(g.at[c, xr, i], xl_r.at[i])
        x_far_left(i).start()
        sib_send(i, xl).start()
        sib_send(i, xr).start()

    def stage_x3(i):
        take(g.at[c, xo, i, 0], xfr_r.at[i])
        take(g.at[c, xo, i, 1], xfl_r.at[i])
        sib_send(i, xo).start()

    def p_send(i):
        return rc(pb.at[i, oc], sb.at[i], ps_s.at[i], ps_r.at[i], sibling)

    def stage_c(i):
        take(g.at[oc, :, i], sib_r.at[i])
        blocks = [g[c_, x_, i].reshape(ROWS, WIDE) for x_ in range(NX) for c_ in range(2)]
        xs = jnp.concatenate([b[:, :FEAT] for b in blocks], axis=1)
        dys = jnp.concatenate([b[:, FEAT : 2 * FEAT] for b in blocks], axis=1)
        xs_buf[i] = xs
        dy_buf[i] = dys
        gg = jnp.dot(xs, wg[...], preferred_element_type=F32)
        u = jnp.dot(xs, wu[...], preferred_element_type=F32)
        h = jnp.dot(dys, wdt[...], preferred_element_type=F32)
        p = gate[i]
        s = jax.nn.sigmoid(gg)
        gs = gg * s
        h = p * h
        abuf[i] = (p * gs * u).astype(BF16)
        d_gate = (h * u * s * (1.0 + gg * (1.0 - s))).astype(BF16)
        d_up = (h * gs).astype(BF16)
        dgbuf[i] = d_gate
        dubuf[i] = d_up
        dd = jnp.concatenate([d_gate, d_up], axis=1)
        for x_ in range(NX):
            piece = jnp.dot(dd, w_in[x_], preferred_element_type=F32).astype(BF16)
            pb[i, 0, x_] = piece[:HALF]
            pb[i, 1, x_] = piece[HALF:]
        p_send(i).start()

    quarter = HALF // 2

    def a_right(i):
        return rc(q.at[i, xo, pl.ds(0, quarter)], rl.at[i], ar_s.at[i], ar_r.at[i], xright)

    def a_left(i):
        return rc(q.at[i, xo, pl.ds(quarter, quarter)], rr.at[i], al_s.at[i], al_r.at[i], xleft)

    def b_right(i):
        return rc(q.at[i, xr], fl.at[i], br_s.at[i], br_r.at[i], xright)

    def b_left(i):
        return rc(q.at[i, xl], fr.at[i], bl_s.at[i], bl_r.at[i], xleft)

    def stage_r1(i):
        take(sb.at[i], ps_r.at[i])
        q[i] = (pb[i, c].astype(F32) + sb[i].astype(F32)).astype(BF16)
        a_right(i).start()
        a_left(i).start()

    def stage_r2(i):
        take(rl.at[i], ar_r.at[i])
        lo, hi = pl.ds(0, quarter), pl.ds(quarter, quarter)
        q[i, xr, lo] = (q[i, xr, lo].astype(F32) + rl[i].astype(F32)).astype(BF16)
        b_right(i).start()
        take(rr.at[i], al_r.at[i])
        q[i, xl, hi] = (q[i, xl, hi].astype(F32) + rr[i].astype(F32)).astype(BF16)
        b_left(i).start()

    def ret_send(i, d, sem):
        to = (y + d) % NY
        return rc(
            back.at[i, slot_rows(to), :], ret.at[i, slot_rows(y), :],
            sem, ret_r, dev(x, c, to, ret_z(i)),
        )

    def stage_r3(i):
        take(fl.at[i], br_r.at[i])
        take(fr.at[i], bl_r.at[i])
        back[i] = (q[i, x].astype(F32) + fl[i].astype(F32) + fr[i].astype(F32)).astype(BF16)
        for d in range(1, NY):
            ret_send(i, d, ret_s.at[i]).start()
        local = (c == 0) & (i == 0)

        @pl.when(local)
        def _():
            pltpu.make_async_copy(
                back.at[i, slot_rows(y), :], ret.at[i, slot_rows(y), :], ret_r
            ).start()

        @pl.when(jnp.logical_not(local))
        def _():
            ret_send(i, 0, ret0_s.at[i]).start()

    stages = (
        (stage_z, 0), (stage_x1, 1), (stage_x2, 2), (stage_x3, 3),
        (stage_c, 4), (stage_r1, 5), (stage_r2, 6), (stage_r3, 7),
    )

    def prepare_in():
        for copy in weights:
            copy.wait()
        for n, w in enumerate((wg, wu)):
            wide = jnp.concatenate(
                [w[...].astype(F32), jnp.zeros((WIDE - 2 * FEAT, HID), F32)], axis=0
            )
            for x_ in range(NX):
                rows = wide[2 * FEAT * x_ : 2 * FEAT * x_ + WIDE].astype(BF16)
                w_in[x_, n * HID : (n + 1) * HID] = rows.T

    over_rows = (((0,), (0,)), ((), ()))

    def flat(ref):
        return ref[...].reshape(CHUNKS * ROWS, ref.shape[-1])

    def over_slots(a, b, out):
        out[...] = lax.dot_general(
            flat(a), flat(b), over_rows, preferred_element_type=F32
        ).astype(BF16)

    extra = {
        0: lambda: pl.loop(0, CHUNKS)(prepare_gate),
        1: prepare_in,
        CHUNKS + LAG - 3: lambda: over_slots(xs_buf, dgbuf, gg_out),
        CHUNKS + LAG - 2: lambda: over_slots(xs_buf, dubuf, gu_out),
        CHUNKS + LAG - 1: lambda: over_slots(dy_buf, abuf, gd_out),
    }

    @pl.loop(0, CHUNKS + LAG)
    def _(step):
        for stage, lag in stages:
            i = step - lag

            @pl.when((i >= 0) & (i < CHUNKS))
            def _():
                stage(i)

        for at, work in extra.items():
            pl.when(step == at)(work)

    order = lax.broadcasted_iota(jnp.int32, (CHUNKS * NY, TOK), 0)
    step_of, y_of = order >> 2, order & (NY - 1)
    dist = far(step_of)
    from_z = jnp.where(c == 0, z + dist, z + NZ - 1 - dist) & (NZ - 1)
    sender = from_z * NY + y_of
    own = ids[ex]
    hit = jnp.zeros((CHUNKS * NY, TOK), F32)
    for k in range(TOP):
        hit = hit + jnp.where(own[k : k + 1] == sender, F32(1.0), F32(0.0))
    back_hot = jnp.where(one_hot(hit, CHUNKS * NY), F32(1.0), F32(0.0)).astype(BF16)
    take(ret, ret_r)
    fin[0] = lax.dot_general(
        ret[...].reshape(CHUNKS * HALF, WIDE), back_hot, over_rows, preferred_element_type=F32
    )
    last = rc(fin.at[0], fin.at[1], fin_s, fin_r, sibling)
    last.start()

    @pl.loop(0, CHUNKS)
    def _(i):
        @pl.when(i < CHUNKS - 2)
        def _():
            z_left(i).wait_send()

            @pl.when(i > 0)
            def _():
                z_right(i).wait_send()

        take(yb.at[i, :, pl.ds(0, (NY - 1) * SLOTS), :], y_s.at[i])
        x_right(i).wait_send()
        x_left(i).wait_send()
        x_far_right(i).wait_send()
        x_far_left(i).wait_send()
        take(g.at[c, :, i], sib_s.at[i])
        p_send(i).wait_send()
        a_right(i).wait_send()
        a_left(i).wait_send()
        b_right(i).wait_send()
        b_left(i).wait_send()
        take(back.at[i, pl.ds(0, (NY - 1) * SLOTS), :], ret_s.at[i])

        @pl.when((c == 1) | (i > 0))
        def _():
            ret_send(i, 0, ret0_s.at[i]).wait_send()

    for copy in first:
        copy.wait_send()
    last.wait()
    total = fin[0] + fin[1]
    gi_out[...] = jnp.where(c == 0, total[:FEAT], total[FEAT : 2 * FEAT]).astype(BF16)


def on_device(x_stash, out_grad, expert_ids, gates, scales, w_gate, w_up, w_down):
    blocks = NZ * NY
    d = 2 * NX * FEAT

    def by_block(a):
        return a.reshape(TOP, blocks, TOK).transpose(1, 0, 2)

    vmem = pl.BlockSpec(memory_space=pltpu.VMEM)
    hbm = pl.BlockSpec(memory_space=pl.ANY)
    block = (CHUNKS, 2, HALF, WIDE)
    dma = pltpu.SemaphoreType.DMA
    per_chunk = dma((CHUNKS,))
    grad_input, grad_gate, grad_up, grad_down = pl.pallas_call(
        kernel,
        out_shape=(
            jax.ShapeDtypeStruct((FEAT, TOK), BF16),
            jax.ShapeDtypeStruct((d, HID), BF16),
            jax.ShapeDtypeStruct((d, HID), BF16),
            jax.ShapeDtypeStruct((d, HID), BF16),
        ),
        in_specs=[vmem] * 5 + [hbm] * 3,
        out_specs=(vmem,) * 4,
        scratch_shapes=[
            pltpu.VMEM((d, HID), BF16),
            pltpu.VMEM((d, HID), BF16),
            pltpu.VMEM((d, HID), BF16),
            pltpu.VMEM((NX, 2 * HID, WIDE), BF16),
            pltpu.VMEM((CHUNKS, ROWS, TOK), BF16),
            pltpu.VMEM((CHUNKS, ROWS, 1), F32),
            pltpu.VMEM((CHUNKS, ROWS, d), BF16),
            pltpu.VMEM((CHUNKS, ROWS, d), BF16),
            pltpu.VMEM((CHUNKS, TOK, WIDE), BF16),
            pltpu.VMEM((CHUNKS, TOK, WIDE), BF16),
            pltpu.VMEM(block, BF16),
            pltpu.VMEM((2, NX) + block, BF16),
            pltpu.VMEM((CHUNKS, ROWS, HID), BF16),
            pltpu.VMEM((CHUNKS, ROWS, HID), BF16),
            pltpu.VMEM((CHUNKS, ROWS, HID), BF16),
            pltpu.VMEM((CHUNKS, 2, NX, HALF, WIDE), BF16),
            pltpu.VMEM((CHUNKS, NX, HALF, WIDE), BF16),
            pltpu.VMEM((CHUNKS, NX, HALF, WIDE), BF16),
            pltpu.VMEM((CHUNKS, HALF // 2, WIDE), BF16),
            pltpu.VMEM((CHUNKS, HALF // 2, WIDE), BF16),
            pltpu.VMEM((CHUNKS, HALF, WIDE), BF16),
            pltpu.VMEM((CHUNKS, HALF, WIDE), BF16),
            pltpu.VMEM((CHUNKS, HALF, WIDE), BF16),
            pltpu.VMEM((CHUNKS, HALF, WIDE), BF16),
            pltpu.VMEM((2, WIDE, TOK), F32),
            dma((3,)),
        ]
        + [per_chunk] * 26
        + [per_chunk, per_chunk, dma, dma, dma],
        compiler_params=pltpu.CompilerParams(
            collective_id=0, has_side_effects=True, vmem_limit_bytes=56 * 1024 * 1024
        ),
    )(
        x_stash.T, out_grad.T, by_block(expert_ids), by_block(gates), scales.reshape(blocks, TOK),
        w_gate[0], w_up[0], w_down[0].T,
    )
    return grad_input.T, grad_gate[None], grad_up[None], grad_down.T[None]


def solution(mesh):
    return jax.shard_map(
        on_device,
        mesh=mesh,
        in_specs=(
            P("expert", "dp"),
            P("expert", "dp"),
            P(),
            P(),
            P(),
            P("expert", None, "dp"),
            P("expert", None, "dp"),
            P("expert", "dp", None),
        ),
        out_specs=(
            P("expert", "dp"),
            P("expert", None, "dp"),
            P("expert", None, "dp"),
            P("expert", "dp", None),
        ),
        check_vma=False,
    )
```

```python
import jax
import jax.numpy as jnp
from jax import lax
from jax.experimental import pallas as pl
from jax.experimental.pallas import tpu as pltpu
from jax.sharding import PartitionSpec as P

TOP = 4
NX, NY, NZ = 4, 4, 16
CHUNKS = NZ // 2
TOK = 128
SLOTS = 16
FEAT = 180
WIDE = 384
HID = 256
HALF = NY * SLOTS
ROWS = 2 * HALF
LAG = 6
PARTS = 2
F32 = jnp.float32
BF16 = jnp.bfloat16


def one_hot(hit, rows):
    tri = (
        lax.broadcasted_iota(jnp.int32, (TOK, TOK), 0)
        < lax.broadcasted_iota(jnp.int32, (TOK, TOK), 1)
    ).astype(BF16)
    rank = jnp.dot(hit.astype(BF16), tri, preferred_element_type=F32)
    code = jnp.where(hit > 0.0, rank, F32(-1.0))
    code = jnp.broadcast_to(code[:, None, :], (rows, SLOTS, TOK)).reshape(rows * SLOTS, TOK)
    slot = lax.broadcasted_iota(jnp.int32, (rows * SLOTS, TOK), 0) & (SLOTS - 1)
    return code == slot.astype(F32)


def far(i):
    return i


def kernel(
    x_in, dy_in, ids, gates, scales, wg_hbm, wu_hbm, wd_hbm,
    gi_out, gg_out, gu_out, gd_out,
    wg, wu, wdt, w_in, sel, gate, xs_buf, dy_buf,
    zp, zm, yb, g, dgbuf, dubuf, abuf, pb, sb, q, rl, rr, fl, fr, back, ret, fin, grads,
    w_sem, out_sem, zp_s, zp_r, zm_s, zm_r, y_s, y_r, xr_s, xr_r, xl_s, xl_r, xfr_s, xfr_r, xfl_s, xfl_r,
    sib_s, sib_r, ps_s, ps_r, ar_s, ar_r, al_s, al_r, br_s, br_r, bl_s, bl_r,
    ret_s, ret0_s, ret_r, fin_s, fin_r,
):
    dp = lax.axis_index("dp")
    ex = lax.axis_index("expert")
    x, c = dp // 2, dp % 2
    z, y = ex // NY, ex % NY
    oc = 1 - c
    xr, xl, xo = (x + 1) % NX, (x + NX - 1) % NX, (x + 2) % NX

    def dev(x_, c_, y_, z_):
        return {"dp": x_ * 2 + c_, "expert": z_ * NY + y_}

    zright, zleft = dev(x, c, y, (z + 1) % NZ), dev(x, c, y, (z + NZ - 1) % NZ)
    xright, xleft = dev(xr, c, y, z), dev(xl, c, y, z)
    sibling = dev(x, oc, y, z)

    def ret_z(i):
        return jnp.where(c == 0, z + NZ - far(i), z + far(i) + 1) % NZ

    def ret_from(i):
        return jnp.where(c == 0, z + far(i), z + NZ - far(i) - 1) % NZ

    def rc(src, dst, s, r, to):
        return pltpu.make_async_remote_copy(
            src_ref=src, dst_ref=dst, send_sem=s, recv_sem=r, device_id=to,
            device_id_type=pl.DeviceIdType.MESH,
        )

    def take(ref, sem):
        pltpu.make_async_copy(ref, ref, sem).wait()

    weights = [
        pltpu.make_async_copy(src, dst, w_sem.at[n])
        for n, (src, dst) in enumerate(((wg_hbm, wg), (wu_hbm, wu), (wd_hbm, wdt)))
    ]
    for copy in weights:
        copy.start()

    barrier = pltpu.get_barrier_semaphore()
    for to in (zright, zleft, xright, xleft, sibling):
        pl.semaphore_signal(barrier, inc=1, device_id=to, device_id_type=pl.DeviceIdType.MESH)
    for d in range(1, NY):
        pl.semaphore_signal(
            barrier, inc=1, device_id=dev(x, c, (y + d) % NY, z),
            device_id_type=pl.DeviceIdType.MESH,
        )

    xs_own = (x_in[...].astype(F32) * scales[pl.ds(ex, 1), :]).astype(BF16).astype(F32)
    own = [xs_own, dy_in[...].astype(F32), jnp.zeros((WIDE - 2 * FEAT, TOK), F32)]
    zp[0] = jnp.concatenate(own, axis=0).astype(BF16).T

    pl.semaphore_wait(barrier, 5 + NY - 1)

    def part(n):
        return pl.ds(n * (TOK // PARTS), TOK // PARTS)

    def z_right(i, n):
        return rc(
            zp.at[i, part(n)], zp.at[i + 1, part(n)], zp_s.at[i, n], zp_r.at[i + 1, n], zright
        )

    def z_left(i, n):
        return rc(
            zm.at[i, part(n)], zm.at[i + 1, part(n)], zm_s.at[i, n], zm_r.at[i + 1, n], zleft
        )

    def z_first(n):
        return rc(
            zp.at[0, part(n)], zm.at[0, part(n)], zm_s.at[CHUNKS - 1, n], zm_r.at[0, n], zleft
        )

    for n in range(PARTS):
        z_first(n).start()
        z_right(0, n).start()

    def origins(i):
        return (z + NZ - far(i)) % NZ, (z + far(i) + 1) % NZ

    def prepare_sel(i):
        expert = z * NY + lax.broadcasted_iota(jnp.int32, (NY, TOK), 0)
        hits = []
        for zo in origins(i):
            block = ids[zo * NY + y]
            hit = jnp.zeros((NY, TOK), F32)
            for k in range(TOP):
                hit = hit + jnp.where(block[k : k + 1] == expert, F32(1.0), F32(0.0))
            hits.append(hit)
        hot = one_hot(jnp.concatenate(hits, axis=0), 2 * NY)
        sel[i] = jnp.where(hot, F32(1.0), F32(0.0)).astype(BF16)

    def prepare_gate(i):
        hits, weight = [], []
        for zo in origins(i):
            for ys in range(NY):
                named = ids[zo * NY + ys] == ex
                hits.append(jnp.sum(jnp.where(named, F32(1.0), F32(0.0)), axis=0, keepdims=True))
                weight.append(
                    jnp.sum(
                        jnp.where(named, gates[zo * NY + ys], F32(0.0)), axis=0, keepdims=True
                    )
                )
        hot = one_hot(jnp.concatenate(hits, axis=0), 2 * NY)
        w = jnp.concatenate(weight, axis=0)
        w = jnp.broadcast_to(w[:, None, :], (2 * NY, SLOTS, TOK)).reshape(ROWS, TOK)
        gate[i] = jnp.sum(jnp.where(hot, w, F32(0.0)), axis=1, keepdims=True)

    pl.loop(0, CHUNKS)(prepare_sel)

    def slot_rows(which):
        return pl.ds(pl.multiple_of(which * SLOTS, SLOTS), SLOTS)

    def y_send(i, d):
        to = (y + d) % NY
        return rc(
            yb.at[i, :, slot_rows(to), :], g.at[c, x, i, :, slot_rows(y), :],
            y_s.at[i], y_r.at[i], dev(x, c, to, z),
        )

    def stage_z(i):
        for n in range(PARTS):
            take(zm.at[i, part(n)], zm_r.at[i, n])

            @pl.when(i < CHUNKS - 1)
            def _():
                z_left(i, n).start()

            @pl.when(i > 0)
            def _():
                take(zp.at[i, part(n)], zp_r.at[i, n])

                @pl.when(i < CHUNKS - 1)
                def _():
                    z_right(i, n).start()

        for h, src in ((0, zp), (1, zm)):
            yb[i, h] = jnp.dot(
                sel[i, pl.ds(h * HALF, HALF)], src[i], preferred_element_type=F32
            ).astype(BF16)
        for d in range(1, NY):
            y_send(i, d).start()
        pltpu.make_async_copy(
            yb.at[i, :, slot_rows(y), :], g.at[c, x, i, :, slot_rows(y), :], y_r.at[i]
        ).start()

    def sib_send(i, x_):
        return rc(g.at[c, x_, i], g.at[c, x_, i], sib_s.at[i], sib_r.at[i], sibling)

    def x_right(i):
        return rc(g.at[c, x, i], g.at[c, x, i], xr_s.at[i], xr_r.at[i], xright)

    def x_left(i):
        return rc(g.at[c, x, i], g.at[c, x, i], xl_s.at[i], xl_r.at[i], xleft)

    def x_far_right(i):
        return rc(g.at[c, xl, i, 0], g.at[c, xl, i, 0], xfr_s.at[i], xfr_r.at[i], xright)

    def x_far_left(i):
        return rc(g.at[c, xr, i, 1], g.at[c, xr, i, 1], xfl_s.at[i], xfl_r.at[i], xleft)

    def stage_x1(i):
        take(g.at[c, x, i], y_r.at[i])
        x_right(i).start()
        x_left(i).start()
        sib_send(i, x).start()

    def stage_x2(i):
        take(g.at[c, xl, i], xr_r.at[i])
        x_far_right(i).start()
        take(g.at[c, xr, i], xl_r.at[i])
        x_far_left(i).start()
        sib_send(i, xl).start()
        sib_send(i, xr).start()

    def stage_x3(i):
        take(g.at[c, xo, i, 0], xfr_r.at[i])
        take(g.at[c, xo, i, 1], xfl_r.at[i])
        sib_send(i, xo).start()

    def p_send(i):
        return rc(pb.at[i, oc], sb.at[i], ps_s.at[i], ps_r.at[i], sibling)

    def stage_c(i):
        take(g.at[oc, :, i], sib_r.at[i])
        blocks = [g[c_, x_, i].reshape(ROWS, WIDE) for x_ in range(NX) for c_ in range(2)]
        xs = jnp.concatenate([b[:, :FEAT] for b in blocks], axis=1)
        dys = jnp.concatenate([b[:, FEAT : 2 * FEAT] for b in blocks], axis=1)
        xs_buf[i] = xs
        dy_buf[i] = dys
        gg = jnp.dot(xs, wg[...], preferred_element_type=F32)
        u = jnp.dot(xs, wu[...], preferred_element_type=F32)
        h = jnp.dot(dys, wdt[...], preferred_element_type=F32)
        p = gate[i]
        s = jax.nn.sigmoid(gg)
        gs = gg * s
        h = p * h
        abuf[i] = (p * gs * u).astype(BF16)
        d_gate = (h * u * s * (1.0 + gg * (1.0 - s))).astype(BF16)
        d_up = (h * gs).astype(BF16)
        dgbuf[i] = d_gate
        dubuf[i] = d_up
        dd = jnp.concatenate([d_gate, d_up], axis=1)
        for x_ in range(NX):
            piece = jnp.dot(dd, w_in[x_], preferred_element_type=F32).astype(BF16)
            pb[i, 0, x_] = piece[:HALF]
            pb[i, 1, x_] = piece[HALF:]
        p_send(i).start()

    quarter = HALF // 2

    def a_right(i):
        return rc(q.at[i, xo, pl.ds(0, quarter)], rl.at[i], ar_s.at[i], ar_r.at[i], xright)

    def a_left(i):
        return rc(q.at[i, xo, pl.ds(quarter, quarter)], rr.at[i], al_s.at[i], al_r.at[i], xleft)

    def b_right(i):
        return rc(q.at[i, xr], fl.at[i], br_s.at[i], br_r.at[i], xright)

    def b_left(i):
        return rc(q.at[i, xl], fr.at[i], bl_s.at[i], bl_r.at[i], xleft)

    def stage_r1(i):
        take(sb.at[i], ps_r.at[i])
        q[i] = (pb[i, c].astype(F32) + sb[i].astype(F32)).astype(BF16)
        a_right(i).start()
        a_left(i).start()

    def stage_r2(i):
        take(rl.at[i], ar_r.at[i])
        lo, hi = pl.ds(0, quarter), pl.ds(quarter, quarter)
        q[i, xr, lo] = (q[i, xr, lo].astype(F32) + rl[i].astype(F32)).astype(BF16)
        b_right(i).start()
        take(rr.at[i], al_r.at[i])
        q[i, xl, hi] = (q[i, xl, hi].astype(F32) + rr[i].astype(F32)).astype(BF16)
        b_left(i).start()

    def ret_send(i, d, sem):
        to = (y + d) % NY
        return rc(
            back.at[i, slot_rows(to), :], ret.at[i, slot_rows(y), :],
            sem, ret_r, dev(x, c, to, ret_z(i)),
        )

    def stage_r3(i):
        take(fl.at[i], br_r.at[i])
        take(fr.at[i], bl_r.at[i])
        back[i] = (q[i, x].astype(F32) + fl[i].astype(F32) + fr[i].astype(F32)).astype(BF16)
        for d in range(1, NY):
            ret_send(i, d, ret_s.at[i]).start()
        local = (c == 0) & (i == 0)

        @pl.when(local)
        def _():
            pltpu.make_async_copy(
                back.at[i, slot_rows(y), :], ret.at[i, slot_rows(y), :], ret_r
            ).start()

        @pl.when(jnp.logical_not(local))
        def _():
            ret_send(i, 0, ret0_s.at[i]).start()

    stages = (
        (stage_z, 0), (stage_x1, 1), (stage_x2, 2), (stage_x3, 3),
        (stage_r1, 4), (stage_r2, 5), (stage_r3, 6), (stage_c, 3),
    )

    def prepare_in():
        for copy in weights:
            copy.wait()
        for n, w in enumerate((wg, wu)):
            wide = jnp.concatenate(
                [w[...].astype(F32), jnp.zeros((WIDE - 2 * FEAT, HID), F32)], axis=0
            )
            for x_ in range(NX):
                rows = wide[2 * FEAT * x_ : 2 * FEAT * x_ + WIDE].astype(BF16)
                w_in[x_, n * HID : (n + 1) * HID] = rows.T

    over_rows = (((0,), (0,)), ((), ()))

    def flat(ref):
        return ref[...].reshape(CHUNKS * ROWS, ref.shape[-1])

    def grad_copy(n):
        return pltpu.make_async_copy(grads.at[n], (gg_out, gu_out, gd_out)[n], out_sem.at[n])

    def over_slots(a, b, n):
        grads[n] = lax.dot_general(
            flat(a), flat(b), over_rows, preferred_element_type=F32
        ).astype(BF16)
        grad_copy(n).start()

    extra = {
        0: lambda: pl.loop(0, CHUNKS)(prepare_gate),
        1: prepare_in,
        CHUNKS + LAG - 2: lambda: over_slots(xs_buf, dgbuf, 0),
        CHUNKS + LAG - 1: lambda: over_slots(xs_buf, dubuf, 1),
    }

    @pl.loop(0, CHUNKS + LAG)
    def _(step):
        for stage, lag in stages:
            i = step - lag

            @pl.when((i >= 0) & (i < CHUNKS))
            def _():
                stage(i)

            if stage is stage_c:
                for at, work in extra.items():
                    pl.when(step == at)(work)

    over_slots(dy_buf, abuf, 2)

    order = lax.broadcasted_iota(jnp.int32, (CHUNKS * NY, TOK), 0)
    step_of, y_of = order >> 2, order & (NY - 1)
    dist = far(step_of)
    from_z = jnp.where(c == 0, z + dist, z + NZ - 1 - dist) & (NZ - 1)
    sender = from_z * NY + y_of
    own = ids[ex]
    hit = jnp.zeros((CHUNKS * NY, TOK), F32)
    for k in range(TOP):
        hit = hit + jnp.where(own[k : k + 1] == sender, F32(1.0), F32(0.0))
    back_hot = jnp.where(one_hot(hit, CHUNKS * NY), F32(1.0), F32(0.0)).astype(BF16)
    take(ret, ret_r)
    fin[0] = lax.dot_general(
        ret[...].reshape(CHUNKS * HALF, WIDE), back_hot, over_rows, preferred_element_type=F32
    )
    last = rc(fin.at[0], fin.at[1], fin_s, fin_r, sibling)
    last.start()

    @pl.loop(0, CHUNKS)
    def _(i):
        @pl.when(i < CHUNKS - 1)
        def _():
            for n in range(PARTS):
                z_left(i, n).wait_send()
                z_right(i, n).wait_send()

        take(yb.at[i, :, pl.ds(0, (NY - 1) * SLOTS), :], y_s.at[i])
        x_right(i).wait_send()
        x_left(i).wait_send()
        x_far_right(i).wait_send()
        x_far_left(i).wait_send()
        take(g.at[c, :, i], sib_s.at[i])
        p_send(i).wait_send()
        a_right(i).wait_send()
        a_left(i).wait_send()
        b_right(i).wait_send()
        b_left(i).wait_send()
        take(back.at[i, pl.ds(0, (NY - 1) * SLOTS), :], ret_s.at[i])

        @pl.when((c == 1) | (i > 0))
        def _():
            ret_send(i, 0, ret0_s.at[i]).wait_send()

    for n in range(PARTS):
        z_first(n).wait_send()
    for n in range(3):
        grad_copy(n).wait()
    last.wait()
    total = fin[0] + fin[1]
    gi_out[...] = jnp.where(c == 0, total[:FEAT], total[FEAT : 2 * FEAT]).astype(BF16)


def hand_over(*refs):
    for n in range(4):
        refs[n + 4][...] = refs[n][...]


def on_device(x_stash, out_grad, expert_ids, gates, scales, w_gate, w_up, w_down):
    blocks = NZ * NY
    d = 2 * NX * FEAT

    def by_block(a):
        return a.reshape(TOP, blocks, TOK).transpose(1, 0, 2)

    vmem = pl.BlockSpec(memory_space=pltpu.VMEM)
    hbm = pl.BlockSpec(memory_space=pl.ANY)
    block = (CHUNKS, 2, HALF, WIDE)
    dma = pltpu.SemaphoreType.DMA
    per_chunk = dma((CHUNKS,))
    results = pl.pallas_call(
        kernel,
        out_shape=(
            jax.ShapeDtypeStruct((FEAT, TOK), BF16),
            jax.ShapeDtypeStruct((d, HID), BF16),
            jax.ShapeDtypeStruct((d, HID), BF16),
            jax.ShapeDtypeStruct((d, HID), BF16),
        ),
        in_specs=[vmem] * 5 + [hbm] * 3,
        out_specs=(vmem, hbm, hbm, hbm),
        scratch_shapes=[
            pltpu.VMEM((d, HID), BF16),
            pltpu.VMEM((d, HID), BF16),
            pltpu.VMEM((d, HID), BF16),
            pltpu.VMEM((NX, 2 * HID, WIDE), BF16),
            pltpu.VMEM((CHUNKS, ROWS, TOK), BF16),
            pltpu.VMEM((CHUNKS, ROWS, 1), F32),
            pltpu.VMEM((CHUNKS, ROWS, d), BF16),
            pltpu.VMEM((CHUNKS, ROWS, d), BF16),
            pltpu.VMEM((CHUNKS, TOK, WIDE), BF16),
            pltpu.VMEM((CHUNKS, TOK, WIDE), BF16),
            pltpu.VMEM(block, BF16),
            pltpu.VMEM((2, NX) + block, BF16),
            pltpu.VMEM((CHUNKS, ROWS, HID), BF16),
            pltpu.VMEM((CHUNKS, ROWS, HID), BF16),
            pltpu.VMEM((CHUNKS, ROWS, HID), BF16),
            pltpu.VMEM((CHUNKS, 2, NX, HALF, WIDE), BF16),
            pltpu.VMEM((CHUNKS, NX, HALF, WIDE), BF16),
            pltpu.VMEM((CHUNKS, NX, HALF, WIDE), BF16),
            pltpu.VMEM((CHUNKS, HALF // 2, WIDE), BF16),
            pltpu.VMEM((CHUNKS, HALF // 2, WIDE), BF16),
            pltpu.VMEM((CHUNKS, HALF, WIDE), BF16),
            pltpu.VMEM((CHUNKS, HALF, WIDE), BF16),
            pltpu.VMEM((CHUNKS, HALF, WIDE), BF16),
            pltpu.VMEM((CHUNKS, HALF, WIDE), BF16),
            pltpu.VMEM((2, WIDE, TOK), F32),
            pltpu.VMEM((3, d, HID), BF16),
            dma((3,)),
            dma((3,)),
        ]
        + [dma((CHUNKS, PARTS))] * 4
        + [per_chunk] * 22
        + [per_chunk, per_chunk, dma, dma, dma],
        compiler_params=pltpu.CompilerParams(
            collective_id=0, has_side_effects=True, vmem_limit_bytes=56 * 1024 * 1024
        ),
    )(
        x_stash.T, out_grad.T, by_block(expert_ids), by_block(gates), scales.reshape(blocks, TOK),
        w_gate[0], w_up[0], w_down[0].T,
    )
    grad_input, grad_gate, grad_up, grad_down = pl.pallas_call(
        hand_over,
        out_shape=tuple(jax.ShapeDtypeStruct(r.shape, r.dtype) for r in results),
        in_specs=[vmem] * 4,
        out_specs=(vmem,) * 4,
    )(*results)
    return grad_input.T, grad_gate[None], grad_up[None], grad_down.T[None]


def solution(mesh):
    return jax.shard_map(
        on_device,
        mesh=mesh,
        in_specs=(
            P("expert", "dp"),
            P("expert", "dp"),
            P(),
            P(),
            P(),
            P("expert", None, "dp"),
            P("expert", None, "dp"),
            P("expert", "dp", None),
        ),
        out_specs=(
            P("expert", "dp"),
            P("expert", None, "dp"),
            P("expert", None, "dp"),
            P("expert", "dp", None),
        ),
        check_vma=False,
    )
```

```python
import functools

import jax
import jax.numpy as jnp
from jax import lax
from jax.experimental import pallas as pl
from jax.experimental.pallas import tpu as pltpu
from jax.sharding import PartitionSpec as P

TOP = 4
NX, NY, NZ = 4, 4, 16
CHUNKS = NZ // 2
TOK = 128
SLOTS = 16
FEAT = 180
WIDE = 384
HID = 256
HALF = NY * SLOTS
ROWS = 2 * HALF
PARTS = 2
DIRECT_X = 8
LATE = 1
DIRECT_R = 5
F32 = jnp.float32
BF16 = jnp.bfloat16


def one_hot(hit, rows):
    tri = (
        lax.broadcasted_iota(jnp.int32, (TOK, TOK), 0)
        < lax.broadcasted_iota(jnp.int32, (TOK, TOK), 1)
    ).astype(BF16)
    rank = jnp.dot(hit.astype(BF16), tri, preferred_element_type=F32)
    code = jnp.where(hit > 0.0, rank, F32(-1.0))
    code = jnp.broadcast_to(code[:, None, :], (rows, SLOTS, TOK)).reshape(rows * SLOTS, TOK)
    slot = lax.broadcasted_iota(jnp.int32, (rows * SLOTS, TOK), 0) & (SLOTS - 1)
    return code == slot.astype(F32)


def far(i):
    return jnp.where(i == CHUNKS - 1, LATE, i + (i >= LATE).astype(jnp.int32))


def kernel(
    x_in, dy_in, ids, gates, scales, wg_hbm, wu_hbm, wd_hbm,
    gi_out, gg_out, gu_out, gd_out,
    wg, wu, wdt, w_in, sel, gate, xs_buf, dy_buf,
    zp, zm, yb, g, dgbuf, dubuf, abuf, pb, sb, q, rl, rr, fl, fr, back, ret, fin, grads,
    w_sem, out_sem, zp_s, zp_r, zm_s, zm_r, y_s, y_r, xr_s, xr_r, xl_s, xl_r, xfr_s, xfr_r, xfl_s, xfl_r,
    sib_s, sib_r, ps_s, ps_r, ar_s, ar_r, al_s, al_r, br_s, br_r, bl_s, bl_r,
    ret_s, ret0_s, ret_r, fin_s, fin_r,
):
    dp = lax.axis_index("dp")
    ex = lax.axis_index("expert")
    x, c = dp // 2, dp % 2
    z, y = ex // NY, ex % NY
    oc = 1 - c
    xr, xl, xo = (x + 1) % NX, (x + NX - 1) % NX, (x + 2) % NX

    def dev(x_, c_, y_, z_):
        return {"dp": x_ * 2 + c_, "expert": z_ * NY + y_}

    zright, zleft = dev(x, c, y, (z + 1) % NZ), dev(x, c, y, (z + NZ - 1) % NZ)
    xright, xleft = dev(xr, c, y, z), dev(xl, c, y, z)
    sibling = dev(x, oc, y, z)

    def ret_z(i):
        return jnp.where(c == 0, z + NZ - far(i), z + far(i) + 1) % NZ

    def ret_from(i):
        return jnp.where(c == 0, z + far(i), z + NZ - far(i) - 1) % NZ

    def rc(src, dst, s, r, to):
        return pltpu.make_async_remote_copy(
            src_ref=src, dst_ref=dst, send_sem=s, recv_sem=r, device_id=to,
            device_id_type=pl.DeviceIdType.MESH,
        )

    def take(ref, sem):
        pltpu.make_async_copy(ref, ref, sem).wait()

    weights = [
        pltpu.make_async_copy(src, dst, w_sem.at[n])
        for n, (src, dst) in enumerate(((wg_hbm, wg), (wu_hbm, wu), (wd_hbm, wdt)))
    ]
    for copy in weights:
        copy.start()

    barrier = pltpu.get_barrier_semaphore()
    xfar = dev(xo, c, y, z)
    for to in (zright, zleft, xright, xleft, xfar, sibling):
        pl.semaphore_signal(barrier, inc=1, device_id=to, device_id_type=pl.DeviceIdType.MESH)
    for d in range(1, NY):
        pl.semaphore_signal(
            barrier, inc=1, device_id=dev(x, c, (y + d) % NY, z),
            device_id_type=pl.DeviceIdType.MESH,
        )

    xs_own = (x_in[...].astype(F32) * scales[pl.ds(ex, 1), :]).astype(BF16).astype(F32)
    own = [xs_own, dy_in[...].astype(F32), jnp.zeros((WIDE - 2 * FEAT, TOK), F32)]
    zp[0] = jnp.concatenate(own, axis=0).astype(BF16).T

    pl.semaphore_wait(barrier, 6 + NY - 1)

    def part(n):
        return pl.ds(n * (TOK // PARTS), TOK // PARTS)

    def z_right(i, n):
        return rc(
            zp.at[i, part(n)], zp.at[i + 1, part(n)], zp_s.at[i, n], zp_r.at[i + 1, n], zright
        )

    def z_left(i, n):
        return rc(
            zm.at[i, part(n)], zm.at[i + 1, part(n)], zm_s.at[i, n], zm_r.at[i + 1, n], zleft
        )

    def z_first(n):
        return rc(
            zp.at[0, part(n)], zm.at[0, part(n)], zm_s.at[CHUNKS - 1, n], zm_r.at[0, n], zleft
        )

    for n in range(PARTS):
        z_first(n).start()
        z_right(0, n).start()

    def origins(i):
        return (z + NZ - far(i)) % NZ, (z + far(i) + 1) % NZ

    def prepare_sel(i):
        expert = z * NY + lax.broadcasted_iota(jnp.int32, (NY, TOK), 0)
        hits = []
        for zo in origins(i):
            block = ids[zo * NY + y]
            hit = jnp.zeros((NY, TOK), F32)
            for k in range(TOP):
                hit = hit + jnp.where(block[k : k + 1] == expert, F32(1.0), F32(0.0))
            hits.append(hit)
        hot = one_hot(jnp.concatenate(hits, axis=0), 2 * NY)
        sel[i] = jnp.where(hot, F32(1.0), F32(0.0)).astype(BF16)

    def prepare_gate(i):
        hits, weight = [], []
        for zo in origins(i):
            for ys in range(NY):
                named = ids[zo * NY + ys] == ex
                hits.append(jnp.sum(jnp.where(named, F32(1.0), F32(0.0)), axis=0, keepdims=True))
                weight.append(
                    jnp.sum(
                        jnp.where(named, gates[zo * NY + ys], F32(0.0)), axis=0, keepdims=True
                    )
                )
        hot = one_hot(jnp.concatenate(hits, axis=0), 2 * NY)
        w = jnp.concatenate(weight, axis=0)
        w = jnp.broadcast_to(w[:, None, :], (2 * NY, SLOTS, TOK)).reshape(ROWS, TOK)
        gate[i] = jnp.sum(jnp.where(hot, w, F32(0.0)), axis=1, keepdims=True)

    pl.loop(0, CHUNKS)(prepare_sel)

    def slot_rows(which):
        return pl.ds(pl.multiple_of(which * SLOTS, SLOTS), SLOTS)

    def y_send(i, d):
        to = (y + d) % NY
        return rc(
            yb.at[i, :, slot_rows(to), :], g.at[c, x, i, :, slot_rows(y), :],
            y_s.at[i], y_r.at[i], dev(x, c, to, z),
        )

    def stage_ring(i):
        for n in range(PARTS):
            take(zm.at[i, part(n)], zm_r.at[i, n])

            @pl.when(i < CHUNKS - 1)
            def _():
                z_left(i, n).start()

            @pl.when(i > 0)
            def _():
                take(zp.at[i, part(n)], zp_r.at[i, n])

                @pl.when(i < CHUNKS - 1)
                def _():
                    z_right(i, n).start()

    def stage_z(i):
        for h, src in ((0, zp), (1, zm)):
            yb[i, h] = jnp.dot(
                sel[i, pl.ds(h * HALF, HALF)], src[far(i)], preferred_element_type=F32
            ).astype(BF16)
        for d in range(1, NY):
            y_send(i, d).start()
        pltpu.make_async_copy(
            yb.at[i, :, slot_rows(y), :], g.at[c, x, i, :, slot_rows(y), :], y_r.at[i]
        ).start()

    def sib_send(i, x_):
        return rc(g.at[c, x_, i], g.at[c, x_, i], sib_s.at[i], sib_r.at[i], sibling)

    def x_right(i, h):
        return rc(g.at[c, x, i, h], g.at[c, x, i, h], xr_s.at[i, h], xr_r.at[i, h], xright)

    def x_left(i, h):
        return rc(g.at[c, x, i, h], g.at[c, x, i, h], xl_s.at[i, h], xl_r.at[i, h], xleft)

    def x_far_right(i):
        return rc(g.at[c, xl, i, 0], g.at[c, xl, i, 0], xfr_s.at[i], xfr_r.at[i], xright)

    def x_far_left(i):
        return rc(g.at[c, xr, i, 1], g.at[c, xr, i, 1], xfl_s.at[i], xfl_r.at[i], xleft)

    def x_direct(i, h):
        s, r = ((xfr_s, xfr_r), (xfl_s, xfl_r))[h]
        return rc(g.at[c, x, i, h], g.at[c, x, i, h], s.at[i], r.at[i], xfar)

    def stage_x1(i):
        take(g.at[c, x, i], y_r.at[i])
        x_right(i, 0).start()
        x_left(i, 1).start()
        x_right(i, 1).start()
        x_left(i, 0).start()

        @pl.when(i >= DIRECT_X)
        def _():
            x_direct(i, 0).start()
            x_direct(i, 1).start()

        sib_send(i, x).start()

    def stage_x2(i):
        take(g.at[c, xl, i, 0], xr_r.at[i, 0])
        take(g.at[c, xr, i, 1], xl_r.at[i, 1])

        @pl.when(i < DIRECT_X)
        def _():
            x_far_right(i).start()
            x_far_left(i).start()

    def stage_x3(i):
        pl.when(i >= DIRECT_X)(lambda: stage_x2(i))
        take(g.at[c, xl, i, 1], xr_r.at[i, 1])
        sib_send(i, xl).start()
        take(g.at[c, xr, i, 0], xl_r.at[i, 0])
        sib_send(i, xr).start()
        take(g.at[c, xo, i, 0], xfr_r.at[i])
        take(g.at[c, xo, i, 1], xfl_r.at[i])
        sib_send(i, xo).start()

    def p_send(i):
        return rc(pb.at[i, oc], sb.at[i], ps_s.at[i], ps_r.at[i], sibling)

    def stage_c(i):
        take(g.at[oc, :, i], sib_r.at[i])
        blocks = [g[c_, x_, i].reshape(ROWS, WIDE) for x_ in range(NX) for c_ in range(2)]
        xs = jnp.concatenate([b[:, :FEAT] for b in blocks], axis=1)
        dys = jnp.concatenate([b[:, FEAT : 2 * FEAT] for b in blocks], axis=1)
        xs_buf[i] = xs
        dy_buf[i] = dys
        gg = jnp.dot(xs, wg[...], preferred_element_type=F32)
        u = jnp.dot(xs, wu[...], preferred_element_type=F32)
        h = jnp.dot(dys, wdt[...], preferred_element_type=F32)
        p = gate[i]
        s = jax.nn.sigmoid(gg)
        gs = gg * s
        h = p * h
        abuf[i] = (p * gs * u).astype(BF16)
        d_gate = (h * u * s * (1.0 + gg * (1.0 - s))).astype(BF16)
        d_up = (h * gs).astype(BF16)
        dgbuf[i] = d_gate
        dubuf[i] = d_up
        dd = jnp.concatenate([d_gate, d_up], axis=1)
        for x_ in range(NX):
            piece = jnp.dot(dd, w_in[x_], preferred_element_type=F32).astype(BF16)
            pb[i, 0, x_] = piece[:HALF]
            pb[i, 1, x_] = piece[HALF:]
        p_send(i).start()

    quarter = HALF // 2

    def side(h):
        return pl.ds(h * quarter, quarter)

    def a_right(i, to):
        return rc(q.at[i, xo, side(0)], rl.at[i], ar_s.at[i], ar_r.at[i], to)

    def a_left(i, to):
        return rc(q.at[i, xo, side(1)], rr.at[i], al_s.at[i], al_r.at[i], to)

    def b_right(i, h):
        return rc(q.at[i, xr, side(h)], fl.at[i, side(h)], br_s.at[i, h], br_r.at[i, h], xright)

    def b_left(i, h):
        return rc(q.at[i, xl, side(h)], fr.at[i, side(h)], bl_s.at[i, h], bl_r.at[i, h], xleft)

    def stage_r1(i):
        take(sb.at[i], ps_r.at[i])
        q[i] = (pb[i, c].astype(F32) + sb[i].astype(F32)).astype(BF16)

        @pl.when(i < DIRECT_R)
        def _():
            a_right(i, xright).start()
            a_left(i, xleft).start()

        @pl.when(i >= DIRECT_R)
        def _():
            a_right(i, xfar).start()
            a_left(i, xfar).start()
            b_right(i, 0).start()
            b_left(i, 1).start()

        b_right(i, 1).start()
        b_left(i, 0).start()

    def stage_r2(i):
        take(rl.at[i], ar_r.at[i])
        q[i, xr, side(0)] = (q[i, xr, side(0)].astype(F32) + rl[i].astype(F32)).astype(BF16)
        b_right(i, 0).start()
        take(rr.at[i], al_r.at[i])
        q[i, xl, side(1)] = (q[i, xl, side(1)].astype(F32) + rr[i].astype(F32)).astype(BF16)
        b_left(i, 1).start()

    def ret_send(i, d, sem):
        to = (y + d) % NY
        return rc(
            back.at[i, slot_rows(to), :], ret.at[i, slot_rows(y), :],
            sem, ret_r, dev(x, c, to, ret_z(i)),
        )

    def stage_r3(i):
        for h in range(2):
            take(fl.at[i, side(h)], br_r.at[i, h])
            take(fr.at[i, side(h)], bl_r.at[i, h])
        total = q[i, x].astype(F32) + fl[i].astype(F32) + fr[i].astype(F32)

        @pl.when(i < DIRECT_R)
        def _():
            back[i] = total.astype(BF16)

        @pl.when(i >= DIRECT_R)
        def _():
            take(rl.at[i], ar_r.at[i])
            take(rr.at[i], al_r.at[i])
            across = jnp.concatenate([rl[i].astype(F32), rr[i].astype(F32)], axis=0)
            back[i] = (total + across).astype(BF16)

        for d in range(1, NY):
            ret_send(i, d, ret_s.at[i]).start()
        local = (c == 0) & (i == 0)

        @pl.when(local)
        def _():
            pltpu.make_async_copy(
                back.at[i, slot_rows(y), :], ret.at[i, slot_rows(y), :], ret_r
            ).start()

        @pl.when(jnp.logical_not(local))
        def _():
            ret_send(i, 0, ret0_s.at[i]).start()

    def at_step(lag, *direct):
        return [i + lag - sum(i >= first for first in direct) for i in range(CHUNKS)]

    stages = (
        (stage_z, at_step(0)),
        (stage_x1, at_step(1)),
        (stage_x2, at_step(2)[:DIRECT_X]),
        (stage_x3, at_step(3, DIRECT_X)),
        (stage_r1, at_step(4, DIRECT_X)),
        (stage_r2, at_step(5, DIRECT_X)[:DIRECT_R]),
        (stage_r3, at_step(6, DIRECT_X, DIRECT_R)),
        (stage_c, at_step(3, DIRECT_X)),
    )
    steps = stages[-2][1][-1] + 1

    def prepare_in():
        for copy in weights:
            copy.wait()
        for n, w in enumerate((wg, wu)):
            wide = jnp.concatenate(
                [w[...].astype(F32), jnp.zeros((WIDE - 2 * FEAT, HID), F32)], axis=0
            )
            for x_ in range(NX):
                rows = wide[2 * FEAT * x_ : 2 * FEAT * x_ + WIDE].astype(BF16)
                w_in[x_, n * HID : (n + 1) * HID] = rows.T

    over_rows = (((0,), (0,)), ((), ()))

    def flat(ref):
        return ref[...].reshape(CHUNKS * ROWS, ref.shape[-1])

    def grad_copy(n):
        return pltpu.make_async_copy(grads.at[n], (gg_out, gu_out, gd_out)[n], out_sem.at[n])

    def over_slots(a, b, n):
        grads[n] = lax.dot_general(
            flat(a), flat(b), over_rows, preferred_element_type=F32
        ).astype(BF16)
        grad_copy(n).start()

    extra = {
        0: lambda: pl.loop(0, CHUNKS)(prepare_gate),
        1: prepare_in,
        steps - 2: lambda: over_slots(xs_buf, dgbuf, 0),
        steps - 1: lambda: over_slots(xs_buf, dubuf, 1),
    }

    @pl.loop(0, steps)
    def _(step):
        ring = step + (step >= LATE).astype(jnp.int32)
        pl.when(ring < CHUNKS)(lambda: stage_ring(ring))
        for stage, when in stages:
            if when == list(range(when[0], when[0] + len(when))):
                i = step - when[0]
                pl.when((i >= 0) & (i < len(when)))(functools.partial(stage, i))
            else:
                low = sum((step > t).astype(jnp.int32) for t in when)
                high = sum((step >= t).astype(jnp.int32) for t in when)
                pl.loop(low, high)(stage)

            if stage is stage_c:
                pl.when(step == LATE - 1)(lambda: stage_ring(step + 1))
                for at, work in extra.items():
                    pl.when(step == at)(work)

    over_slots(dy_buf, abuf, 2)

    order = lax.broadcasted_iota(jnp.int32, (CHUNKS * NY, TOK), 0)
    step_of, y_of = order >> 2, order & (NY - 1)
    dist = far(step_of)
    from_z = jnp.where(c == 0, z + dist, z + NZ - 1 - dist) & (NZ - 1)
    sender = from_z * NY + y_of
    own = ids[ex]
    hit = jnp.zeros((CHUNKS * NY, TOK), F32)
    for k in range(TOP):
        hit = hit + jnp.where(own[k : k + 1] == sender, F32(1.0), F32(0.0))
    back_hot = jnp.where(one_hot(hit, CHUNKS * NY), F32(1.0), F32(0.0)).astype(BF16)
    take(ret, ret_r)
    fin[0] = lax.dot_general(
        ret[...].reshape(CHUNKS * HALF, WIDE), back_hot, over_rows, preferred_element_type=F32
    )
    last = rc(fin.at[0], fin.at[1], fin_s, fin_r, sibling)
    last.start()

    @pl.loop(0, CHUNKS)
    def _(i):
        @pl.when(i < CHUNKS - 1)
        def _():
            for n in range(PARTS):
                z_left(i, n).wait_send()
                z_right(i, n).wait_send()

        take(yb.at[i, :, pl.ds(0, (NY - 1) * SLOTS), :], y_s.at[i])
        for h in range(2):
            x_right(i, h).wait_send()
            x_left(i, h).wait_send()
            b_right(i, h).wait_send()
            b_left(i, h).wait_send()
        x_far_right(i).wait_send()
        x_far_left(i).wait_send()
        take(g.at[c, :, i], sib_s.at[i])
        p_send(i).wait_send()
        a_right(i, xright).wait_send()
        a_left(i, xleft).wait_send()
        take(back.at[i, pl.ds(0, (NY - 1) * SLOTS), :], ret_s.at[i])

        @pl.when((c == 1) | (i > 0))
        def _():
            ret_send(i, 0, ret0_s.at[i]).wait_send()

    for n in range(PARTS):
        z_first(n).wait_send()
    for n in range(3):
        grad_copy(n).wait()
    last.wait()
    total = fin[0] + fin[1]
    gi_out[...] = jnp.where(c == 0, total[:FEAT], total[FEAT : 2 * FEAT]).astype(BF16)


def hand_over(*refs):
    ins, outs, held, sem = refs[:4], refs[4:8], refs[8:12], refs[12]
    load = [pltpu.make_async_copy(ins[n], held[n], sem.at[0, n]) for n in range(4)]
    store = [pltpu.make_async_copy(held[n], outs[n], sem.at[1, n]) for n in range(4)]
    for copy in load:
        copy.start()
    for n in range(4):
        load[n].wait()
        store[n].start()
    for copy in store:
        copy.wait()


def on_device(x_stash, out_grad, expert_ids, gates, scales, w_gate, w_up, w_down):
    blocks = NZ * NY
    d = 2 * NX * FEAT

    def by_block(a):
        return a.reshape(TOP, blocks, TOK).transpose(1, 0, 2)

    vmem = pl.BlockSpec(memory_space=pltpu.VMEM)
    hbm = pl.BlockSpec(memory_space=pl.ANY)
    block = (CHUNKS, 2, HALF, WIDE)
    dma = pltpu.SemaphoreType.DMA
    per_chunk = dma((CHUNKS,))
    results = pl.pallas_call(
        kernel,
        out_shape=(
            jax.ShapeDtypeStruct((FEAT, TOK), BF16),
            jax.ShapeDtypeStruct((d, HID), BF16),
            jax.ShapeDtypeStruct((d, HID), BF16),
            jax.ShapeDtypeStruct((d, HID), BF16),
        ),
        in_specs=[vmem] * 5 + [hbm] * 3,
        out_specs=(vmem, hbm, hbm, hbm),
        scratch_shapes=[
            pltpu.VMEM((d, HID), BF16),
            pltpu.VMEM((d, HID), BF16),
            pltpu.VMEM((d, HID), BF16),
            pltpu.VMEM((NX, 2 * HID, WIDE), BF16),
            pltpu.VMEM((CHUNKS, ROWS, TOK), BF16),
            pltpu.VMEM((CHUNKS, ROWS, 1), F32),
            pltpu.VMEM((CHUNKS, ROWS, d), BF16),
            pltpu.VMEM((CHUNKS, ROWS, d), BF16),
            pltpu.VMEM((CHUNKS, TOK, WIDE), BF16),
            pltpu.VMEM((CHUNKS, TOK, WIDE), BF16),
            pltpu.VMEM(block, BF16),
            pltpu.VMEM((2, NX) + block, BF16),
            pltpu.VMEM((CHUNKS, ROWS, HID), BF16),
            pltpu.VMEM((CHUNKS, ROWS, HID), BF16),
            pltpu.VMEM((CHUNKS, ROWS, HID), BF16),
            pltpu.VMEM((CHUNKS, 2, NX, HALF, WIDE), BF16),
            pltpu.VMEM((CHUNKS, NX, HALF, WIDE), BF16),
            pltpu.VMEM((CHUNKS, NX, HALF, WIDE), BF16),
            pltpu.VMEM((CHUNKS, HALF // 2, WIDE), BF16),
            pltpu.VMEM((CHUNKS, HALF // 2, WIDE), BF16),
            pltpu.VMEM((CHUNKS, HALF, WIDE), BF16),
            pltpu.VMEM((CHUNKS, HALF, WIDE), BF16),
            pltpu.VMEM((CHUNKS, HALF, WIDE), BF16),
            pltpu.VMEM((CHUNKS, HALF, WIDE), BF16),
            pltpu.VMEM((2, WIDE, TOK), F32),
            pltpu.VMEM((3, d, HID), BF16),
            dma((3,)),
            dma((3,)),
        ]
        + [dma((CHUNKS, PARTS))] * 4
        + [per_chunk] * 2
        + [dma((CHUNKS, 2))] * 4
        + [per_chunk] * 12
        + [dma((CHUNKS, 2))] * 4
        + [per_chunk, per_chunk, dma, dma, dma],
        compiler_params=pltpu.CompilerParams(
            collective_id=0, has_side_effects=True, vmem_limit_bytes=56 * 1024 * 1024
        ),
    )(
        x_stash.T, out_grad.T, by_block(expert_ids), by_block(gates), scales.reshape(blocks, TOK),
        w_gate[0], w_up[0], w_down[0].T,
    )
    grad_input, grad_gate, grad_up, grad_down = pl.pallas_call(
        hand_over,
        out_shape=tuple(jax.ShapeDtypeStruct(r.shape, r.dtype) for r in results),
        in_specs=[hbm] * 4,
        out_specs=(hbm,) * 4,
        scratch_shapes=[pltpu.VMEM(r.shape, r.dtype) for r in results] + [dma((2, 4))],
        compiler_params=pltpu.CompilerParams(vmem_limit_bytes=60 * 1024 * 1024),
    )(*results)
    return grad_input.T, grad_gate[None], grad_up[None], grad_down.T[None]


def solution(mesh):
    return jax.shard_map(
        on_device,
        mesh=mesh,
        in_specs=(
            P("expert", "dp"),
            P("expert", "dp"),
            P(),
            P(),
            P(),
            P("expert", None, "dp"),
            P("expert", None, "dp"),
            P("expert", "dp", None),
        ),
        out_specs=(
            P("expert", "dp"),
            P("expert", None, "dp"),
            P("expert", None, "dp"),
            P("expert", "dp", None),
        ),
        check_vma=False,
    )
```

```python
import functools

import jax
import jax.numpy as jnp
from jax import lax
from jax.experimental import pallas as pl
from jax.experimental.pallas import tpu as pltpu
from jax.sharding import PartitionSpec as P

TOP = 4
NX, NY, NZ = 4, 4, 16
CHUNKS = NZ // 2
TOK = 128
SLOTS = 16
FEAT = 180
WIDE = 384
HID = 256
HALF = NY * SLOTS
ROWS = 2 * HALF
PARTS = 2
DIRECT_X = 8
LATE = 1
DIRECT_R = 5
F32 = jnp.float32
BF16 = jnp.bfloat16


def one_hot(hit, rows):
    tri = (
        lax.broadcasted_iota(jnp.int32, (TOK, TOK), 0)
        < lax.broadcasted_iota(jnp.int32, (TOK, TOK), 1)
    ).astype(BF16)
    rank = jnp.dot(hit.astype(BF16), tri, preferred_element_type=F32)
    code = jnp.where(hit > 0.0, rank, F32(-1.0))
    code = jnp.broadcast_to(code[:, None, :], (rows, SLOTS, TOK)).reshape(rows * SLOTS, TOK)
    slot = lax.broadcasted_iota(jnp.int32, (rows * SLOTS, TOK), 0) & (SLOTS - 1)
    return code == slot.astype(F32)


def far(i):
    return jnp.where(i == CHUNKS - 1, LATE, i + (i >= LATE).astype(jnp.int32))


def kernel(
    x_in, dy_in, scales, ids_hbm, gates_hbm, wg_hbm, wu_hbm, wd_hbm,
    gi_out, gg_out, gu_out, gd_out,
    ids, gates, wg, wu, wdt, w_in, sel, gate, xs_buf, dy_buf,
    zp, zm, yb, g, dgbuf, dubuf, abuf, pb, sb, q, rl, rr, fl, fr, back, ret, fin, grads,
    w_sem, out_sem, zp_s, zp_r, zm_s, zm_r, y_s, y_r, xr_s, xr_r, xl_s, xl_r, xfr_s, xfr_r, xfl_s, xfl_r,
    sib_s, sib_r, ps_s, ps_r, ar_s, ar_r, al_s, al_r, br_s, br_r, bl_s, bl_r,
    ret_s, ret0_s, ret_r, fin_s, fin_r,
):
    dp = lax.axis_index("dp")
    ex = lax.axis_index("expert")
    x, c = dp // 2, dp % 2
    z, y = ex // NY, ex % NY
    oc = 1 - c
    xr, xl, xo = (x + 1) % NX, (x + NX - 1) % NX, (x + 2) % NX

    def dev(x_, c_, y_, z_):
        return {"dp": x_ * 2 + c_, "expert": z_ * NY + y_}

    zright, zleft = dev(x, c, y, (z + 1) % NZ), dev(x, c, y, (z + NZ - 1) % NZ)
    xright, xleft = dev(xr, c, y, z), dev(xl, c, y, z)
    sibling = dev(x, oc, y, z)

    def ret_z(i):
        return jnp.where(c == 0, z + NZ - far(i), z + far(i) + 1) % NZ

    def ret_from(i):
        return jnp.where(c == 0, z + far(i), z + NZ - far(i) - 1) % NZ

    def rc(src, dst, s, r, to):
        return pltpu.make_async_remote_copy(
            src_ref=src, dst_ref=dst, send_sem=s, recv_sem=r, device_id=to,
            device_id_type=pl.DeviceIdType.MESH,
        )

    def take(ref, sem):
        pltpu.make_async_copy(ref, ref, sem).wait()

    pairs = (
        (ids_hbm, ids), (gates_hbm, gates), (wg_hbm, wg), (wu_hbm, wu), (wd_hbm, wdt),
    )
    tables = [pltpu.make_async_copy(src, dst, w_sem.at[n]) for n, (src, dst) in enumerate(pairs)]
    weights = tables[2:]
    for copy in tables:
        copy.start()

    barrier = pltpu.get_barrier_semaphore()
    xfar = dev(xo, c, y, z)
    for to in (zright, zleft, xright, xleft, xfar, sibling):
        pl.semaphore_signal(barrier, inc=1, device_id=to, device_id_type=pl.DeviceIdType.MESH)
    for d in range(1, NY):
        pl.semaphore_signal(
            barrier, inc=1, device_id=dev(x, c, (y + d) % NY, z),
            device_id_type=pl.DeviceIdType.MESH,
        )

    xs_own = (x_in[...].astype(F32) * scales[pl.ds(ex, 1), :]).astype(BF16).astype(F32)
    own = [xs_own, dy_in[...].astype(F32), jnp.zeros((WIDE - 2 * FEAT, TOK), F32)]
    zp[0] = jnp.concatenate(own, axis=0).astype(BF16).T

    pl.semaphore_wait(barrier, 6 + NY - 1)

    def part(n):
        return pl.ds(n * (TOK // PARTS), TOK // PARTS)

    def z_right(i, n):
        return rc(
            zp.at[i, part(n)], zp.at[i + 1, part(n)], zp_s.at[i, n], zp_r.at[i + 1, n], zright
        )

    def z_left(i, n):
        return rc(
            zm.at[i, part(n)], zm.at[i + 1, part(n)], zm_s.at[i, n], zm_r.at[i + 1, n], zleft
        )

    def z_first(n):
        return rc(
            zp.at[0, part(n)], zm.at[0, part(n)], zm_s.at[CHUNKS - 1, n], zm_r.at[0, n], zleft
        )

    for n in range(PARTS):
        z_first(n).start()
        z_right(0, n).start()

    def origins(i):
        return (z + NZ - far(i)) % NZ, (z + far(i) + 1) % NZ

    def prepare_sel(i):
        expert = z * NY + lax.broadcasted_iota(jnp.int32, (NY, TOK), 0)
        hits = []
        for zo in origins(i):
            block = ids[zo * NY + y]
            hit = jnp.zeros((NY, TOK), F32)
            for k in range(TOP):
                hit = hit + jnp.where(block[k : k + 1] == expert, F32(1.0), F32(0.0))
            hits.append(hit)
        hot = one_hot(jnp.concatenate(hits, axis=0), 2 * NY)
        sel[i] = jnp.where(hot, F32(1.0), F32(0.0)).astype(BF16)

    def prepare_gate(i):
        hits, weight = [], []
        for zo in origins(i):
            for ys in range(NY):
                named = ids[zo * NY + ys] == ex
                hits.append(jnp.sum(jnp.where(named, F32(1.0), F32(0.0)), axis=0, keepdims=True))
                weight.append(
                    jnp.sum(
                        jnp.where(named, gates[zo * NY + ys], F32(0.0)), axis=0, keepdims=True
                    )
                )
        hot = one_hot(jnp.concatenate(hits, axis=0), 2 * NY)
        w = jnp.concatenate(weight, axis=0)
        w = jnp.broadcast_to(w[:, None, :], (2 * NY, SLOTS, TOK)).reshape(ROWS, TOK)
        gate[i] = jnp.sum(jnp.where(hot, w, F32(0.0)), axis=1, keepdims=True)

    for copy in tables[:2]:
        copy.wait()
    pl.loop(0, CHUNKS)(prepare_sel)

    def slot_rows(which):
        return pl.ds(pl.multiple_of(which * SLOTS, SLOTS), SLOTS)

    def y_send(i, d):
        to = (y + d) % NY
        return rc(
            yb.at[i, :, slot_rows(to), :], g.at[c, x, i, :, slot_rows(y), :],
            y_s.at[i], y_r.at[i], dev(x, c, to, z),
        )

    def stage_ring(i):
        for n in range(PARTS):
            take(zm.at[i, part(n)], zm_r.at[i, n])

            @pl.when(i < CHUNKS - 1)
            def _():
                z_left(i, n).start()

            @pl.when(i > 0)
            def _():
                take(zp.at[i, part(n)], zp_r.at[i, n])

                @pl.when(i < CHUNKS - 1)
                def _():
                    z_right(i, n).start()

    def stage_z(i):
        for h, src in ((0, zp), (1, zm)):
            yb[i, h] = jnp.dot(
                sel[i, pl.ds(h * HALF, HALF)], src[far(i)], preferred_element_type=F32
            ).astype(BF16)
        for d in range(1, NY):
            y_send(i, d).start()
        pltpu.make_async_copy(
            yb.at[i, :, slot_rows(y), :], g.at[c, x, i, :, slot_rows(y), :], y_r.at[i]
        ).start()

    def sib_send(i, x_):
        return rc(g.at[c, x_, i], g.at[c, x_, i], sib_s.at[i], sib_r.at[i], sibling)

    def x_right(i, h):
        return rc(g.at[c, x, i, h], g.at[c, x, i, h], xr_s.at[i, h], xr_r.at[i, h], xright)

    def x_left(i, h):
        return rc(g.at[c, x, i, h], g.at[c, x, i, h], xl_s.at[i, h], xl_r.at[i, h], xleft)

    def x_far_right(i):
        return rc(g.at[c, xl, i, 0], g.at[c, xl, i, 0], xfr_s.at[i], xfr_r.at[i], xright)

    def x_far_left(i):
        return rc(g.at[c, xr, i, 1], g.at[c, xr, i, 1], xfl_s.at[i], xfl_r.at[i], xleft)

    def x_direct(i, h):
        s, r = ((xfr_s, xfr_r), (xfl_s, xfl_r))[h]
        return rc(g.at[c, x, i, h], g.at[c, x, i, h], s.at[i], r.at[i], xfar)

    def stage_x1(i):
        take(g.at[c, x, i], y_r.at[i])
        x_right(i, 0).start()
        x_left(i, 1).start()
        x_right(i, 1).start()
        x_left(i, 0).start()

        @pl.when(i >= DIRECT_X)
        def _():
            x_direct(i, 0).start()
            x_direct(i, 1).start()

        sib_send(i, x).start()

    def stage_x2(i):
        take(g.at[c, xl, i, 0], xr_r.at[i, 0])
        take(g.at[c, xr, i, 1], xl_r.at[i, 1])

        @pl.when(i < DIRECT_X)
        def _():
            x_far_right(i).start()
            x_far_left(i).start()

    def stage_x3(i):
        pl.when(i >= DIRECT_X)(lambda: stage_x2(i))
        take(g.at[c, xl, i, 1], xr_r.at[i, 1])
        sib_send(i, xl).start()
        take(g.at[c, xr, i, 0], xl_r.at[i, 0])
        sib_send(i, xr).start()
        take(g.at[c, xo, i, 0], xfr_r.at[i])
        take(g.at[c, xo, i, 1], xfl_r.at[i])
        sib_send(i, xo).start()

    def p_send(i):
        return rc(pb.at[i, oc], sb.at[i], ps_s.at[i], ps_r.at[i], sibling)

    def stage_c(i):
        take(g.at[oc, :, i], sib_r.at[i])
        blocks = [g[c_, x_, i].reshape(ROWS, WIDE) for x_ in range(NX) for c_ in range(2)]
        xs = jnp.concatenate([b[:, :FEAT] for b in blocks], axis=1)
        dys = jnp.concatenate([b[:, FEAT : 2 * FEAT] for b in blocks], axis=1)
        xs_buf[i] = xs
        dy_buf[i] = dys
        gg = jnp.dot(xs, wg[...], preferred_element_type=F32)
        u = jnp.dot(xs, wu[...], preferred_element_type=F32)
        h = jnp.dot(dys, wdt[...], preferred_element_type=F32)
        p = gate[i]
        s = jax.nn.sigmoid(gg)
        gs = gg * s
        h = p * h
        abuf[i] = (p * gs * u).astype(BF16)
        d_gate = (h * u * s * (1.0 + gg * (1.0 - s))).astype(BF16)
        d_up = (h * gs).astype(BF16)
        dgbuf[i] = d_gate
        dubuf[i] = d_up
        dd = jnp.concatenate([d_gate, d_up], axis=1)
        for x_ in range(NX):
            piece = jnp.dot(dd, w_in[x_], preferred_element_type=F32).astype(BF16)
            pb[i, 0, x_] = piece[:HALF]
            pb[i, 1, x_] = piece[HALF:]
        p_send(i).start()

    quarter = HALF // 2

    def side(h):
        return pl.ds(h * quarter, quarter)

    def a_right(i, to):
        return rc(q.at[i, xo, side(0)], rl.at[i], ar_s.at[i], ar_r.at[i], to)

    def a_left(i, to):
        return rc(q.at[i, xo, side(1)], rr.at[i], al_s.at[i], al_r.at[i], to)

    def b_right(i, h):
        return rc(q.at[i, xr, side(h)], fl.at[i, side(h)], br_s.at[i, h], br_r.at[i, h], xright)

    def b_left(i, h):
        return rc(q.at[i, xl, side(h)], fr.at[i, side(h)], bl_s.at[i, h], bl_r.at[i, h], xleft)

    def stage_r1(i):
        take(sb.at[i], ps_r.at[i])
        q[i] = (pb[i, c].astype(F32) + sb[i].astype(F32)).astype(BF16)

        @pl.when(i < DIRECT_R)
        def _():
            a_right(i, xright).start()
            a_left(i, xleft).start()

        @pl.when(i >= DIRECT_R)
        def _():
            a_right(i, xfar).start()
            a_left(i, xfar).start()
            b_right(i, 0).start()
            b_left(i, 1).start()

        b_right(i, 1).start()
        b_left(i, 0).start()

    def stage_r2(i):
        take(rl.at[i], ar_r.at[i])
        q[i, xr, side(0)] = (q[i, xr, side(0)].astype(F32) + rl[i].astype(F32)).astype(BF16)
        b_right(i, 0).start()
        take(rr.at[i], al_r.at[i])
        q[i, xl, side(1)] = (q[i, xl, side(1)].astype(F32) + rr[i].astype(F32)).astype(BF16)
        b_left(i, 1).start()

    def ret_send(i, d, sem):
        to = (y + d) % NY
        return rc(
            back.at[i, slot_rows(to), :], ret.at[i, slot_rows(y), :],
            sem, ret_r, dev(x, c, to, ret_z(i)),
        )

    def stage_r3(i):
        for h in range(2):
            take(fl.at[i, side(h)], br_r.at[i, h])
            take(fr.at[i, side(h)], bl_r.at[i, h])
        total = q[i, x].astype(F32) + fl[i].astype(F32) + fr[i].astype(F32)

        @pl.when(i < DIRECT_R)
        def _():
            back[i] = total.astype(BF16)

        @pl.when(i >= DIRECT_R)
        def _():
            take(rl.at[i], ar_r.at[i])
            take(rr.at[i], al_r.at[i])
            across = jnp.concatenate([rl[i].astype(F32), rr[i].astype(F32)], axis=0)
            back[i] = (total + across).astype(BF16)

        for d in range(1, NY):
            ret_send(i, d, ret_s.at[i]).start()
        local = (c == 0) & (i == 0)

        @pl.when(local)
        def _():
            pltpu.make_async_copy(
                back.at[i, slot_rows(y), :], ret.at[i, slot_rows(y), :], ret_r
            ).start()

        @pl.when(jnp.logical_not(local))
        def _():
            ret_send(i, 0, ret0_s.at[i]).start()

    def at_step(lag, *direct):
        return [i + lag - sum(i >= first for first in direct) for i in range(CHUNKS)]

    stages = (
        (stage_z, at_step(0)),
        (stage_x1, at_step(1)),
        (stage_x2, at_step(2)[:DIRECT_X]),
        (stage_x3, at_step(3, DIRECT_X)),
        (stage_r1, at_step(4, DIRECT_X)),
        (stage_r2, at_step(5, DIRECT_X)[:DIRECT_R]),
        (stage_r3, at_step(6, DIRECT_X, DIRECT_R)),
        (stage_c, at_step(3, DIRECT_X)),
    )
    steps = stages[-2][1][-1] + 1

    def prepare_in():
        for copy in weights:
            copy.wait()
        for n, w in enumerate((wg, wu)):
            wide = jnp.concatenate(
                [w[...].astype(F32), jnp.zeros((WIDE - 2 * FEAT, HID), F32)], axis=0
            )
            for x_ in range(NX):
                rows = wide[2 * FEAT * x_ : 2 * FEAT * x_ + WIDE].astype(BF16)
                w_in[x_, n * HID : (n + 1) * HID] = rows.T

    over_rows = (((0,), (0,)), ((), ()))

    def flat(ref):
        return ref[...].reshape(CHUNKS * ROWS, ref.shape[-1])

    def grad_copy(n):
        return pltpu.make_async_copy(grads.at[n], (gg_out, gu_out, gd_out)[n], out_sem.at[n])

    def over_slots(a, b, n):
        grads[n] = lax.dot_general(
            flat(a), flat(b), over_rows, preferred_element_type=F32
        ).astype(BF16)
        grad_copy(n).start()

    extra = {
        0: lambda: pl.loop(0, CHUNKS)(prepare_gate),
        1: prepare_in,
        steps - 2: lambda: over_slots(xs_buf, dgbuf, 0),
        steps - 1: lambda: over_slots(xs_buf, dubuf, 1),
    }

    @pl.loop(0, steps)
    def _(step):
        ring = step + (step >= LATE).astype(jnp.int32)
        pl.when(ring < CHUNKS)(lambda: stage_ring(ring))
        for stage, when in stages:
            if when == list(range(when[0], when[0] + len(when))):
                i = step - when[0]
                pl.when((i >= 0) & (i < len(when)))(functools.partial(stage, i))
            else:
                low = sum((step > t).astype(jnp.int32) for t in when)
                high = sum((step >= t).astype(jnp.int32) for t in when)
                pl.loop(low, high)(stage)

            if stage is stage_c:
                pl.when(step == LATE - 1)(lambda: stage_ring(step + 1))
                for at, work in extra.items():
                    pl.when(step == at)(work)

    over_slots(dy_buf, abuf, 2)

    order = lax.broadcasted_iota(jnp.int32, (CHUNKS * NY, TOK), 0)
    step_of, y_of = order >> 2, order & (NY - 1)
    dist = far(step_of)
    from_z = jnp.where(c == 0, z + dist, z + NZ - 1 - dist) & (NZ - 1)
    sender = from_z * NY + y_of
    own = ids[ex]
    hit = jnp.zeros((CHUNKS * NY, TOK), F32)
    for k in range(TOP):
        hit = hit + jnp.where(own[k : k + 1] == sender, F32(1.0), F32(0.0))
    back_hot = jnp.where(one_hot(hit, CHUNKS * NY), F32(1.0), F32(0.0)).astype(BF16)
    take(ret, ret_r)
    fin[0] = lax.dot_general(
        ret[...].reshape(CHUNKS * HALF, WIDE), back_hot, over_rows, preferred_element_type=F32
    )
    last = rc(fin.at[0], fin.at[1], fin_s, fin_r, sibling)
    last.start()

    @pl.loop(0, CHUNKS)
    def _(i):
        @pl.when(i < CHUNKS - 1)
        def _():
            for n in range(PARTS):
                z_left(i, n).wait_send()
                z_right(i, n).wait_send()

        take(yb.at[i, :, pl.ds(0, (NY - 1) * SLOTS), :], y_s.at[i])
        for h in range(2):
            x_right(i, h).wait_send()
            x_left(i, h).wait_send()
            b_right(i, h).wait_send()
            b_left(i, h).wait_send()
        x_far_right(i).wait_send()
        x_far_left(i).wait_send()
        take(g.at[c, :, i], sib_s.at[i])
        p_send(i).wait_send()
        a_right(i, xright).wait_send()
        a_left(i, xleft).wait_send()
        take(back.at[i, pl.ds(0, (NY - 1) * SLOTS), :], ret_s.at[i])

        @pl.when((c == 1) | (i > 0))
        def _():
            ret_send(i, 0, ret0_s.at[i]).wait_send()

    for n in range(PARTS):
        z_first(n).wait_send()
    for n in range(3):
        grad_copy(n).wait()
    last.wait()
    total = fin[0] + fin[1]
    gi_out[...] = jnp.where(c == 0, total[:FEAT], total[FEAT : 2 * FEAT]).astype(BF16)


def hand_over(*refs):
    ins, outs, held, sem = refs[:4], refs[4:8], refs[8:12], refs[12]
    load = [pltpu.make_async_copy(ins[n], held[n], sem.at[0, n]) for n in range(4)]
    store = [pltpu.make_async_copy(held[n], outs[n], sem.at[1, n]) for n in range(4)]
    for copy in load:
        copy.start()
    for n in range(4):
        load[n].wait()
        store[n].start()
    for copy in store:
        copy.wait()


def on_device(x_stash, out_grad, expert_ids, gates, scales, w_gate, w_up, w_down):
    blocks = NZ * NY
    d = 2 * NX * FEAT

    def by_block(a):
        return a.reshape(TOP, blocks, TOK).transpose(1, 0, 2)

    vmem = pl.BlockSpec(memory_space=pltpu.VMEM)
    hbm = pl.BlockSpec(memory_space=pl.ANY)
    block = (CHUNKS, 2, HALF, WIDE)
    dma = pltpu.SemaphoreType.DMA
    per_chunk = dma((CHUNKS,))
    results = pl.pallas_call(
        kernel,
        out_shape=(
            jax.ShapeDtypeStruct((FEAT, TOK), BF16),
            jax.ShapeDtypeStruct((d, HID), BF16),
            jax.ShapeDtypeStruct((d, HID), BF16),
            jax.ShapeDtypeStruct((d, HID), BF16),
        ),
        in_specs=[vmem] * 3 + [hbm] * 5,
        out_specs=(vmem, hbm, hbm, hbm),
        scratch_shapes=[
            pltpu.VMEM((blocks, TOP, TOK), jnp.int32),
            pltpu.VMEM((blocks, TOP, TOK), F32),
            pltpu.VMEM((d, HID), BF16),
            pltpu.VMEM((d, HID), BF16),
            pltpu.VMEM((d, HID), BF16),
            pltpu.VMEM((NX, 2 * HID, WIDE), BF16),
            pltpu.VMEM((CHUNKS, ROWS, TOK), BF16),
            pltpu.VMEM((CHUNKS, ROWS, 1), F32),
            pltpu.VMEM((CHUNKS, ROWS, d), BF16),
            pltpu.VMEM((CHUNKS, ROWS, d), BF16),
            pltpu.VMEM((CHUNKS, TOK, WIDE), BF16),
            pltpu.VMEM((CHUNKS, TOK, WIDE), BF16),
            pltpu.VMEM(block, BF16),
            pltpu.VMEM((2, NX) + block, BF16),
            pltpu.VMEM((CHUNKS, ROWS, HID), BF16),
            pltpu.VMEM((CHUNKS, ROWS, HID), BF16),
            pltpu.VMEM((CHUNKS, ROWS, HID), BF16),
            pltpu.VMEM((CHUNKS, 2, NX, HALF, WIDE), BF16),
            pltpu.VMEM((CHUNKS, NX, HALF, WIDE), BF16),
            pltpu.VMEM((CHUNKS, NX, HALF, WIDE), BF16),
            pltpu.VMEM((CHUNKS, HALF // 2, WIDE), BF16),
            pltpu.VMEM((CHUNKS, HALF // 2, WIDE), BF16),
            pltpu.VMEM((CHUNKS, HALF, WIDE), BF16),
            pltpu.VMEM((CHUNKS, HALF, WIDE), BF16),
            pltpu.VMEM((CHUNKS, HALF, WIDE), BF16),
            pltpu.VMEM((CHUNKS, HALF, WIDE), BF16),
            pltpu.VMEM((2, WIDE, TOK), F32),
            pltpu.VMEM((3, d, HID), BF16),
            dma((5,)),
            dma((3,)),
        ]
        + [dma((CHUNKS, PARTS))] * 4
        + [per_chunk] * 2
        + [dma((CHUNKS, 2))] * 4
        + [per_chunk] * 12
        + [dma((CHUNKS, 2))] * 4
        + [per_chunk, per_chunk, dma, dma, dma],
        compiler_params=pltpu.CompilerParams(
            collective_id=0, has_side_effects=True, vmem_limit_bytes=56 * 1024 * 1024
        ),
    )(
        x_stash.T, out_grad.T, scales.reshape(blocks, TOK), by_block(expert_ids), by_block(gates),
        w_gate[0], w_up[0], w_down[0].T,
    )
    grad_input, grad_gate, grad_up, grad_down = pl.pallas_call(
        hand_over,
        out_shape=tuple(jax.ShapeDtypeStruct(r.shape, r.dtype) for r in results),
        in_specs=[hbm] * 4,
        out_specs=(hbm,) * 4,
        scratch_shapes=[pltpu.VMEM(r.shape, r.dtype) for r in results] + [dma((2, 4))],
        compiler_params=pltpu.CompilerParams(vmem_limit_bytes=60 * 1024 * 1024),
    )(*results)
    return grad_input.T, grad_gate[None], grad_up[None], grad_down.T[None]


def solution(mesh):
    return jax.shard_map(
        on_device,
        mesh=mesh,
        in_specs=(
            P("expert", "dp"),
            P("expert", "dp"),
            P(),
            P(),
            P(),
            P("expert", None, "dp"),
            P("expert", None, "dp"),
            P("expert", "dp", None),
        ),
        out_specs=(
            P("expert", "dp"),
            P("expert", None, "dp"),
            P("expert", None, "dp"),
            P("expert", "dp", None),
        ),
        check_vma=False,
    )
```
